32 devices in a mesh: groups: 2 (over y), ctx: 4 (over z), head: 4 (over x, core).
Axes of the slice: x: 2, y: 2, z: 4, core: 2. Of those that a mesh axis runs over, the one named last changes fastest.
Arguments:
- queries: bfloat16 [4096, 4096], P(('groups', 'ctx'), 'head'), parts along dimension 0, may hold values from -40 to 40
- keys: bfloat16 [4096, 4096], P(('groups', 'ctx'), 'head'), parts along dimension 0, may hold values from -4 to 4
- values: bfloat16 [4096, 4096], P(('groups', 'ctx'), 'head'), parts along dimension 0, may hold values from -40 to 40
- log_decay: bfloat16 [4096, 32], P(('groups', 'ctx'), 'head'), parts along dimension 0, may hold values from -1.6 to 0
- arrival_positions: int32 [4096], P(('groups', 'ctx')), parts along dimension 0, may hold values from 0 to 2047, as said below
- prompt_lengths: int32 [8], P('groups'), parts along dimension 0, may hold values from 1 to 1024, 2048 in all
- norm_gain: float32 [4096], P('head'), may hold values from 0.5 to 2
- out_weight: bfloat16 [4096, 6144], P(None, 'head'), may hold values from -0.09375 to 0.09375
Outputs:
- layer_out: bfloat16 [4096, 6144], P(('groups', 'ctx'), 'head'), parts along dimension 0
The draws below stay inside these ranges and needn't reach their ends.
There are 2 independent parts, one for each index of `groups`. The reference program is written for one: setup_inputs(seed, part) draws one part's arguments, and reference() takes and returns one part's arrays. A program takes and returns all parts, laid end to end along the dimension named above; an argument that names none is the same for every part. Nothing has to cross between parts.
Inputs may be any that keep to these rules, and one draw needn't show every extreme that they name: `arrival_positions`: each packed position appears once. The rows that one arrival device holds of one owner are one run of consecutive positions, of 64 or 192 rows, and every arrival device holds such a run of every owner. `prompt_lengths`: they sum to 2048; the longest is exactly 1024.
All inputs are finite; a program needn't handle non-finite values.
Results may differ from the reference program's by a relative error of at most 0.013.
Values may be sent and summed in bfloat16 or wider, within the bound.
No kernel may reach another device: no remote copies, remote signals or barrier semaphores. Data moves between devices by JAX's collectives and lax.ppermute only.
A program may use at most 64 MiB of HBM per device.

```python
import math
import jax
import jax.numpy as jnp
import numpy as np
from jax import lax

D = 6144
HEAD_TOTAL = 32
DH = 128
TOK_DEV = 512
PROMPTS = 4
TOKENS = 2048


def arrival_layout(key):
    owners = TOKENS // TOK_DEV
    unit_rows = TOK_DEV // (2 * owners)
    key_size, key_shift, key_order = jax.random.split(jax.random.fold_in(key, 11), 3)
    base_units = jnp.where(jnp.arange(owners) < owners // 2, 1, 3)
    piece_sizes = unit_rows * base_units[jax.random.permutation(key_size, owners)]
    offsets = jnp.cumsum(piece_sizes) - piece_sizes
    shifts = jax.random.permutation(key_shift, owners)
    orders = jax.vmap(lambda sub_key: jax.random.permutation(sub_key, owners))(jax.random.split(key_order, owners))
    slot_sizes = piece_sizes[orders]
    slot_ends = jnp.cumsum(slot_sizes, axis=1)
    slot_starts = slot_ends - slot_sizes
    row_line = jnp.arange(TOK_DEV)
    slot_of = jnp.sum((row_line[None, :, None] >= slot_ends[:, None, :]).astype(jnp.int32), axis=2)
    piece_of = jnp.take_along_axis(orders, slot_of, axis=1)
    within = row_line[None, :] - jnp.take_along_axis(slot_starts, slot_of, axis=1)
    owner_of = (jnp.arange(owners)[:, None] - shifts[piece_of]) % owners
    return (owner_of * TOK_DEV + offsets[piece_of] + within).reshape(-1).astype(jnp.int32)


def draw_arrival_positions(key, part):
    return arrival_layout(key)


def draw_log_decay(key, part):
    positions = arrival_layout(key)
    random_key_ordering, random_key_quick, random_key_block, random_key_jitter, random_key_location, random_key_cluster = jax.random.split(jax.random.fold_in(key, 23), 6)
    rank_line = jax.random.permutation(random_key_ordering, HEAD_TOTAL)
    fast_heads = HEAD_TOTAL // 2
    rough_low = 0.5
    rough_high = 1.5
    fast_rate = jnp.exp(jax.random.uniform(random_key_quick, (HEAD_TOTAL,), jnp.float32, math.log(1.0 / 50.0), math.log(1.0 / 30.0)))
    head_decay_rate = jnp.where(rank_line < fast_heads, fast_rate, 0.5 / TOKENS)
    owners = TOKENS // TOK_DEV
    block_multiplier = jnp.repeat(jnp.exp(jax.random.uniform(random_key_block, (owners, HEAD_TOTAL), jnp.float32, math.log(0.5), math.log(2.0))), TOK_DEV, axis=0)
    jitter_level = jax.random.uniform(random_key_jitter, (TOKENS, HEAD_TOTAL), jnp.float32, rough_low, rough_high)
    spots = jax.random.randint(random_key_location, (2, HEAD_TOTAL), 0, TOKENS)
    cluster_length = jax.random.uniform(random_key_cluster, (2, HEAD_TOTAL), jnp.float32, math.log(0.5), math.log(0.8))
    match_mask = jnp.arange(TOKENS)[:, None, None] == spots[None, :, :]
    prompt_clusters = jnp.sum(jnp.where(match_mask, cluster_length[None, :, :], 0.0), axis=1)
    packed_tensors = -head_decay_rate[None, :] * block_multiplier * jitter_level + prompt_clusters
    return packed_tensors[positions].astype(jnp.bfloat16)


def draw_queries(key, part):
    key_value, key_scale = jax.random.split(jax.random.fold_in(key, 31), 2)
    base_values = jax.random.truncated_normal(key_value, -4.0, 4.0, (TOKENS, HEAD_TOTAL * DH), jnp.float32)
    top_scale = 10.0
    row_scale = jnp.exp(jax.random.uniform(key_scale, (TOKENS, 1), jnp.float32, 0.0, math.log(top_scale)))
    return (base_values * row_scale).astype(jnp.bfloat16)


def draw_values(key, part):
    key_value, key_scale = jax.random.split(jax.random.fold_in(key, 41), 2)
    base_values = jax.random.truncated_normal(key_value, -4.0, 4.0, (TOKENS, HEAD_TOTAL * DH), jnp.float32)
    column_scale = jnp.exp(jax.random.uniform(key_scale, (1, HEAD_TOTAL * DH), jnp.float32, 0.0, math.log(10.0)))
    return (base_values * column_scale).astype(jnp.bfloat16)


def block_levels(own_key, dims, cuts, least, top_value):
    level = 1.0
    for dim, parts in cuts:
        heights = jax.random.uniform(jax.random.fold_in(jax.random.fold_in(own_key, 6), dim), (parts,), jnp.float32, least / len(cuts), top_value / len(cuts))
        level = level * jnp.repeat(jnp.exp(heights), dims[dim] // parts).reshape((-1,) + (1,) * (len(dims) - 1 - dim))
    return level


def split_up(number_of, total, bound, lean):
    weights = [(1 << 20) // math.isqrt(standing ** lean) + 1 for standing in range(2, number_of + 1)]
    rest, holding = total - bound - (number_of - 1), [1] * (number_of - 1)
    while rest > 0:
        candidates = [i for i in range(number_of - 1) if holding[i] < bound]
        pool, budget = sum([weights[i] for i in candidates]), rest
        for i in candidates:
            addition = min(bound - holding[i], max(1, budget * weights[i] // pool), rest)
            holding[i] = holding[i] + addition
            rest = rest - addition
    return np.array([bound] + holding)


def ragged_sizes(key, count, total, bound, slope):
    if count == 2:
        one = jax.random.randint(key, (), max(1, total - bound), min(bound, total - 1) + 1)
        return jnp.stack([one, total - one])
    sizes = jnp.asarray(split_up(count, total, bound, slope), jnp.int32)
    pairs = (count - 1) // 2
    donor, sink = sizes[1:1 + 2 * pairs:2], sizes[2:2 + 2 * pairs:2]
    margin = jnp.minimum(donor - 1, bound - sink)
    passed = jax.random.randint(jax.random.fold_in(key, 1), (pairs,), 0, 1 << 20) % (margin + 1)
    sizes = sizes.at[1:1 + 2 * pairs:2].set(donor - passed).at[2:2 + 2 * pairs:2].set(sink + passed)
    return sizes[jax.random.permutation(jax.random.fold_in(key, 2), count)]


def scatter_about(stream_key, dims, scale, limit, cuts=(), kind=jnp.bfloat16):
    factor_of = block_levels(stream_key, dims, cuts, -0.22, 0.18) if cuts else 1.0
    result = jax.random.normal(stream_key, dims, jnp.float32) * scale * factor_of
    return jnp.minimum(jnp.maximum(result, -limit), limit).astype(kind)


def setup_inputs(seed: int = 0, part: int = 0) -> dict:
    arg_keys = jax.random.split(jax.random.key(seed), 9)
    part_keys = jax.random.split(jax.random.fold_in(arg_keys[8], part), 9)
    queries = draw_queries(jax.random.fold_in(jax.random.fold_in(arg_keys[8], part), 71), part)
    keys = scatter_about(part_keys[1], (TOKENS, HEAD_TOTAL * DH), 1.0, 4.0, ((0, 4), (1, 4)))
    values = draw_values(jax.random.fold_in(jax.random.fold_in(arg_keys[8], part), 71), part)
    log_decay = draw_log_decay(jax.random.fold_in(jax.random.fold_in(arg_keys[8], part), 71), part)
    arrival_positions = draw_arrival_positions(jax.random.fold_in(jax.random.fold_in(arg_keys[8], part), 71), part)
    prompt_lengths = ragged_sizes(part_keys[5], PROMPTS, TOKENS, TOKENS // 2, 2).astype(jnp.int32)
    norm_gain = jnp.clip(jnp.exp(math.log(2.0) - 1.3862944 * jax.random.uniform(arg_keys[6], (HEAD_TOTAL * DH,), jnp.float32) ** block_levels(arg_keys[6], (HEAD_TOTAL * DH,), ((0, 4),), -0.2, 0.2)), 0.5, 2.0)
    out_weight = scatter_about(arg_keys[7], (HEAD_TOTAL * DH, D), (HEAD_TOTAL * DH) ** -0.5, 0.09375, ((1, 4),))
    return dict(queries=queries, keys=keys, values=values, log_decay=log_decay, arrival_positions=arrival_positions, prompt_lengths=prompt_lengths, norm_gain=norm_gain, out_weight=out_weight)


def block_step(carry, block):
    run_state, last_cum, last_seg = carry
    block_q, block_k, block_v, block_cum, block_seg = block
    query_f = block_q.astype(jnp.float32)
    key_f = block_k.astype(jnp.float32)
    value_f = block_v.astype(jnp.float32)
    linked = block_seg == last_seg
    reach_back = jnp.where(linked[:, None], jnp.exp(block_cum - last_cum[None, :]), 0.0)
    earlier = jnp.einsum('thd,hde->the', query_f, run_state, precision=lax.Precision.HIGHEST) * reach_back[:, :, None]
    block_rows = block_seg.shape[0]
    order_ok = jnp.arange(block_rows)[:, None] >= jnp.arange(block_rows)[None, :]
    allowed = order_ok & (block_seg[:, None] == block_seg[None, :])
    by_head = block_cum.T
    spread = by_head[:, :, None] - by_head[:, None, :]
    decay_table = jnp.where(allowed[None], jnp.exp(jnp.where(allowed[None], spread, 0.0)), 0.0)
    scores = jnp.einsum('thd,shd->hts', query_f, key_f, precision=lax.Precision.HIGHEST)
    inside = jnp.einsum('hts,shd->thd', scores * decay_table, value_f, precision=lax.Precision.HIGHEST)
    end_seg = block_seg[-1]
    toward = jnp.where((block_seg == end_seg)[:, None], jnp.exp(block_cum[-1][None, :] - block_cum), 0.0)
    local_state = jnp.einsum('shd,she->hde', key_f * toward[:, :, None], value_f, precision=lax.Precision.HIGHEST)
    keep_factor = jnp.where(jnp.all(linked), jnp.exp(block_cum[-1] - last_cum), 0.0)
    new_state = keep_factor[:, None, None] * run_state + local_state
    return ((new_state, block_cum[-1], end_seg), earlier + inside)

def reference(queries, keys, values, log_decay, arrival_positions, prompt_lengths, norm_gain, out_weight):
    row_order = jnp.argsort(arrival_positions)
    packed_q = queries[row_order].reshape(TOKENS, HEAD_TOTAL, DH)
    packed_k = keys[row_order].reshape(TOKENS, HEAD_TOTAL, DH)
    packed_v = values[row_order].reshape(TOKENS, HEAD_TOTAL, DH)
    packed_decay = log_decay[row_order].astype(jnp.float32)
    cumulative = jnp.cumsum(packed_decay, axis=0)
    positions = jnp.arange(TOKENS, dtype=jnp.int32)
    prompt_ends = jnp.cumsum(prompt_lengths)[:-1].astype(jnp.int32)
    segment = lax.optimization_barrier(jnp.sum((positions[:, None] >= prompt_ends[None, :]).astype(jnp.int32), axis=1)).astype(jnp.int32)
    block_size = math.gcd(TOKENS, 512)
    block_count = TOKENS // block_size
    blocks = (packed_q.reshape(block_count, block_size, HEAD_TOTAL, DH), packed_k.reshape(block_count, block_size, HEAD_TOTAL, DH), packed_v.reshape(block_count, block_size, HEAD_TOTAL, DH), cumulative.reshape(block_count, block_size, HEAD_TOTAL), segment.reshape(block_count, block_size))
    start_carry = (jnp.zeros((HEAD_TOTAL, DH, DH), jnp.float32), jnp.zeros((HEAD_TOTAL,), jnp.float32), jnp.int32(-1))
    final_carry, attention = lax.scan(block_step, start_carry, blocks)
    attention = attention.reshape(TOKENS, HEAD_TOTAL, DH)
    inv_scale = lax.rsqrt(lax.optimization_barrier(jnp.mean(attention * attention, axis=-1, keepdims=True)) + 1e-06)
    normed = (attention * inv_scale * norm_gain.reshape(HEAD_TOTAL, DH)).astype(jnp.bfloat16).reshape(TOKENS, HEAD_TOTAL * DH)
    return jnp.dot(normed, out_weight, preferred_element_type=jnp.float32).astype(jnp.bfloat16)
```

```python
import functools
import math

import jax
import jax.numpy as jnp
from jax import lax
from jax.experimental import pallas as pl
from jax.experimental.pallas import tpu as pltpu
from jax.sharding import PartitionSpec as P


LANES = 128
META = 16
CHUNK = 256
CUT = -256.0
VMEM_LIMIT = 60 * 1024 * 1024


def mxu(a, b, dims=((1,), (0,))):
    return lax.dot_general(a, b, (dims, ((), ())), preferred_element_type=jnp.float32)


def pack_kernel(
    owners, half, me_ref, pos_ref, decay_ref, q_hbm, k_hbm, v_hbm, *refs
):
    outs, (buffers, sems) = refs[:owners], refs[owners:]
    rows = q_hbm.shape[0]
    width = owners * LANES
    span = pl.ds(half * width, width)
    copies = [
        pltpu.make_async_copy(ref.at[:, span], buffers.at[n], sems.at[n])
        for n, ref in enumerate((k_hbm, v_hbm, q_hbm))
    ]
    for copy in copies:
        copy.start()
    unit = rows // (2 * owners)
    pos_row = pos_ref[...].astype(jnp.float32)
    pos_col = jnp.transpose(jnp.broadcast_to(pos_row, (LANES, rows)))[:, 0:1]
    rank = jnp.sum((pos_col < pos_row).astype(jnp.float32), axis=0, keepdims=True)
    place = lax.broadcasted_iota(jnp.int32, (rows, rows), 0).astype(jnp.float32)
    order = (place == rank).astype(jnp.bfloat16)
    heads = decay_ref.shape[0]
    unit_row = (pos_row * (1.0 / unit)).astype(jnp.int32).astype(jnp.float32)
    spare = jnp.zeros((META - 1 - heads, rows), jnp.float32)
    aux = jnp.concatenate([decay_ref[...].astype(jnp.float32), spare, unit_row], axis=0)
    meta = mxu(aux.astype(jnp.bfloat16), order, ((1,), (1,)))
    line = lax.broadcasted_iota(jnp.int32, (META, LANES), 0)
    row_id = lax.broadcasted_iota(jnp.int32, (META, rows), 0)
    units = meta[META - 1 : META, :]
    pieces = rows // LANES
    for shift in range(owners):
        head = half * owners + lax.rem(me_ref[0] + shift, owners)
        decay = jnp.sum(jnp.where(row_id == head, meta, 0.0), axis=0, keepdims=True)
        block = jnp.zeros((META, LANES), jnp.float32)
        for n in range(pieces):
            part = slice(n * LANES, (n + 1) * LANES)
            block = jnp.where(line == n, decay[:, part], block)
            block = jnp.where(line == pieces + n, units[:, part], block)
        outs[shift][3 * rows : 3 * rows + META, :] = block.astype(jnp.bfloat16)
    for n, slot in enumerate((1, 2, 0)):
        copies[n].wait()
        ordered = mxu(order, buffers[n]).astype(jnp.bfloat16)
        buffers[n] = ordered
        for shift in range(owners):
            peer = lax.rem(me_ref[0] + shift, owners)
            cols = pl.ds(pl.multiple_of(peer * LANES, LANES), LANES)
            outs[shift][slot * rows : (slot + 1) * rows, :] = buffers[n, :, cols]


def pack(owners, half, me, positions, log_decay, queries, keys, values):
    rows = queries.shape[0]
    width = owners * LANES
    out = jax.ShapeDtypeStruct((3 * rows + META, LANES), jnp.bfloat16)
    vmem = pl.BlockSpec(memory_space=pltpu.VMEM)
    hbm = pl.BlockSpec(memory_space=pltpu.HBM)
    return pl.pallas_call(
        functools.partial(pack_kernel, owners, half),
        out_shape=[out] * owners,
        in_specs=[pl.BlockSpec(memory_space=pltpu.SMEM), vmem, vmem, hbm, hbm, hbm],
        out_specs=[vmem] * owners,
        scratch_shapes=[
            pltpu.VMEM((3, rows, width), jnp.bfloat16),
            pltpu.SemaphoreType.DMA((3,)),
        ],
        compiler_params=pltpu.CompilerParams(vmem_limit_bytes=VMEM_LIMIT),
        cost_estimate=pl.CostEstimate(
            flops=2 * rows * rows * width * 3, bytes_accessed=rows * width * 12, transcendentals=0
        ),
        name="pack_rows",
    )(me, positions, log_decay, queries, keys, values)


def split_pair(source):
    upper = source.astype(jnp.bfloat16)
    return upper, (source - upper.astype(jnp.float32)).astype(jnp.bfloat16)


def attend_kernel(owners, unit, me_ref, table_ref, ends_ref, gain_ref, *refs):
    blocks, outs = refs[:owners], refs[owners : 2 * owners]
    q_all, k_all, v_all, d_all, n_all = refs[2 * owners :]
    rows = outs[0].shape[0]
    tokens = owners * rows
    per_block = rows // unit
    pieces = rows // LANES
    for s in range(owners):
        meta = blocks[s][3 * rows : 3 * rows + META, :].astype(jnp.float32)
        square = jnp.concatenate([meta, jnp.zeros((LANES - META, LANES), jnp.float32)], axis=0)
        columns = jnp.transpose(square)
        for u in range(per_block):
            to = pl.ds(pl.multiple_of(table_ref[s * per_block + u] * unit, unit), unit)
            here = u * unit
            q_all[to, :] = blocks[s][here : here + unit, :]
            k_all[to, :] = blocks[s][rows + here : rows + here + unit, :]
            v_all[to, :] = blocks[s][2 * rows + here : 2 * rows + here + unit, :]
            piece, first = here // LANES, here % LANES
            d_all[to, :] = jnp.broadcast_to(
                columns[first : first + unit, piece : piece + 1], (unit, LANES)
            )
    chunk = min(CHUNK, tokens)
    row_line = lax.broadcasted_iota(jnp.int32, (chunk, chunk), 0)
    col_line = lax.broadcasted_iota(jnp.int32, (chunk, chunk), 1)
    causal = row_line >= col_line
    lower = causal.astype(jnp.bfloat16)
    place = lax.broadcasted_iota(jnp.int32, (chunk, LANES), 0)
    gain = gain_ref[...]
    state = jnp.zeros((LANES, LANES), jnp.float32)
    for c in range(tokens // chunk):
        base = c * chunk
        span = slice(base, base + chunk)
        q, k, v = q_all[span, :], k_all[span, :], v_all[span, :]
        decay = d_all[span, :]
        for j in range(ends_ref.shape[0]):
            decay = jnp.where(place + base == ends_ref[j], CUT, decay)
        total = mxu(lower, decay.astype(jnp.bfloat16))
        across = jnp.transpose(total)[0:1, :]
        wide = jnp.concatenate([total] * (chunk // LANES), axis=1)
        table = jnp.exp(jnp.where(causal, wide - across, -1e30))
        scores = mxu(q, k, ((1,), (1,)))
        inside = mxu((scores * table).astype(jnp.bfloat16), v)
        out = inside
        if c > 0:
            upper, lowpart = split_pair(state)
            out = out + (mxu(q, upper) + mxu(q, lowpart)) * jnp.exp(total)
        last = total[chunk - 1 : chunk, :]
        toward = (k.astype(jnp.float32) * jnp.exp(last - total)).astype(jnp.bfloat16)
        grown = mxu(toward, v, ((0,), (0,)))
        state = jnp.exp(last) * state + grown if c > 0 else grown
        scale = lax.rsqrt(jnp.mean(out * out, axis=1, keepdims=True) + 1e-06)
        n_all[span, :] = (out * scale * gain).astype(jnp.bfloat16)
    for s in range(owners):
        owner = lax.rem(me_ref[0] + s, owners)
        outs[s][...] = n_all[pl.ds(pl.multiple_of(owner * rows, rows), rows), :]


def attend_heads(owners, rows, unit, me, table, ends, gain, blocks):
    tokens = owners * rows
    out = jax.ShapeDtypeStruct((rows, LANES), jnp.bfloat16)
    smem = pl.BlockSpec(memory_space=pltpu.SMEM)
    vmem = pl.BlockSpec(memory_space=pltpu.VMEM)
    return pl.pallas_call(
        functools.partial(attend_kernel, owners, unit),
        out_shape=[out] * owners,
        in_specs=[smem, smem, smem, vmem] + [vmem] * owners,
        out_specs=[vmem] * owners,
        scratch_shapes=[
            pltpu.VMEM((tokens, LANES), jnp.bfloat16),
            pltpu.VMEM((tokens, LANES), jnp.bfloat16),
            pltpu.VMEM((tokens, LANES), jnp.bfloat16),
            pltpu.VMEM((tokens, LANES), jnp.float32),
            pltpu.VMEM((tokens, LANES), jnp.bfloat16),
        ],
        compiler_params=pltpu.CompilerParams(vmem_limit_bytes=VMEM_LIMIT),
        cost_estimate=pl.CostEstimate(
            flops=tokens * LANES * 2 * (2 * CHUNK + 4 * LANES),
            bytes_accessed=tokens * LANES * 8,
            transcendentals=tokens * CHUNK,
        ),
        name="attend_heads",
    )(me, table, ends, gain, *blocks)


def project_kernel(owners, count, carried, scalars_ref, *refs):
    parts, weights, rest = refs[:count], refs[count : 2 * count], refs[2 * count :]
    out, joined = rest[-2:]
    rows = out.shape[0]

    @pl.when(pl.program_id(0) == 0)
    def _():
        for n in range(count):
            for s in range(owners):
                head = lax.rem(scalars_ref[0] + owners - s, owners)
                cols = pl.ds(pl.multiple_of(head * LANES, LANES), LANES)
                joined[n, :, cols] = parts[n][s * rows : (s + 1) * rows, :]

    total = rest[0][...] if carried else None
    for n in range(count):
        term = mxu(joined[n], weights[n][...])
        total = term if total is None else total + term
    out[...] = total.astype(out.dtype)


def project(owners, scalars, parts, weight, carried, dtype):
    count = len(parts)
    rows = parts[0].shape[0] // owners
    depth = owners * LANES
    width = weight.shape[1]
    tile = math.gcd(width, 256)
    block = pl.BlockSpec((rows, tile), lambda i, scalars: (0, i))
    extra = [] if carried is None else [carried]
    weights = [
        pl.BlockSpec((depth, tile), lambda i, scalars, n=n: (scalars[1 + n], i))
        for n in range(count)
    ]
    return pl.pallas_call(
        functools.partial(project_kernel, owners, count, carried is not None),
        out_shape=jax.ShapeDtypeStruct((rows, width), dtype),
        grid_spec=pltpu.PrefetchScalarGridSpec(
            num_scalar_prefetch=1,
            grid=(width // tile,),
            in_specs=[pl.BlockSpec(memory_space=pltpu.VMEM)] * count
            + weights
            + [block] * len(extra),
            out_specs=block,
            scratch_shapes=[pltpu.VMEM((count, rows, depth), jnp.bfloat16)],
        ),
        compiler_params=pltpu.CompilerParams(vmem_limit_bytes=VMEM_LIMIT),
        cost_estimate=pl.CostEstimate(
            flops=2 * count * rows * depth * width,
            bytes_accessed=count * depth * width * 2 + rows * width * 4,
            transcendentals=0,
        ),
        name="project",
    )(scalars, *parts, *([weight] * count), *extra)


def shift_pairs(count, shift):
    return [(a, (a + shift) % count) for a in range(count)]


def local_by_heads(
    queries, keys, values, log_decay, arrival_positions, prompt_lengths, norm_gain, out_weight
):
    rows = queries.shape[0]
    heads = log_decay.shape[1]
    owners = lax.axis_size("ctx")
    columns = lax.axis_size("head")
    unit = rows // (2 * owners)
    halves = heads // owners
    index = lax.axis_index("ctx")
    me = index.astype(jnp.int32).reshape(1)
    positions = arrival_positions[None, :]
    ends = jnp.cumsum(prompt_lengths)[:-1].astype(jnp.int32)
    gains = norm_gain.reshape(halves, owners, LANES)
    gain = lax.dynamic_slice_in_dim(gains, index, 1, axis=1)

    def exchange(blocks, behind):
        got = [blocks[0]]
        for s in range(1, owners):
            block = blocks[s]
            if behind is not None:
                block, behind[s] = lax.optimization_barrier((block, behind[s]))
            got.append(lax.ppermute(block, "ctx", shift_pairs(owners, s)))
        return got

    received = []
    for half in range(halves):
        sent = pack(owners, half, me, positions, log_decay.T, queries, keys, values)
        received.append(exchange(sent, received[-1] if received else None))
    pieces = rows // LANES
    table = jnp.concatenate(
        [
            block[3 * rows + pieces : 3 * rows + 2 * pieces, :].reshape(rows)[::unit]
            for block in received[0]
        ]
    ).astype(jnp.int32)
    mine = lax.axis_index("head")

    def run(group, total, dtype):
        blocks = [(mine ^ flip) * halves + half for flip, half, _ in group]
        scalars = jnp.stack([index] + blocks).astype(jnp.int32)
        return project(owners, scalars, [part for _, _, part in group], out_weight, total, dtype)

    def flip_head(part, flip):
        return lax.ppermute(part, "head", [(a, a ^ flip) for a in range(columns)])

    behind = received[-1]
    group, total = [], None
    for half in range(halves):
        sent = attend_heads(owners, rows, unit, me, table, ends, gain[half], received[half])
        behind = exchange(sent, behind)
        normed = jnp.concatenate(behind, axis=0)
        last = half == halves - 1
        group += [(0, half, normed), (1, half, flip_head(normed, 1))]
        for far in range(2, columns, 2):
            across = flip_head(normed, far)
            if last and far == 2:
                total = run(group, total, jnp.float32)
                group = []
                total, across = lax.optimization_barrier((total, across))
            group += [(far, half, across), (far + 1, half, flip_head(across, 1))]
    total = run(group, total, jnp.bfloat16)
    return total


def split_terms(source):
    upper_part = source.astype(jnp.bfloat16)
    lower_part = (source - upper_part.astype(jnp.float32)).astype(jnp.bfloat16)
    return (upper_part, lower_part)


def paired_einsum(form, wide_operand, narrow_operand, wide_first):
    upper_part, lower_part = split_terms(wide_operand)
    if wide_first:
        return jnp.einsum(
            form, upper_part, narrow_operand, preferred_element_type=jnp.float32
        ) + jnp.einsum(form, lower_part, narrow_operand, preferred_element_type=jnp.float32)
    return jnp.einsum(
        form, narrow_operand, upper_part, preferred_element_type=jnp.float32
    ) + jnp.einsum(form, narrow_operand, lower_part, preferred_element_type=jnp.float32)


def block_terms(run_state, last_seg, block_q, block_k, block_v, block_cum, block_seg):
    linked = block_seg == last_seg
    reach_back = jnp.where(linked[:, None], jnp.exp(block_cum), 0.0)
    earlier = paired_einsum("thd,hde->the", run_state, block_q, False) * reach_back[:, :, None]
    block_rows = block_seg.shape[0]
    order_ok = jnp.arange(block_rows)[:, None] >= jnp.arange(block_rows)[None, :]
    allowed = order_ok & (block_seg[:, None] == block_seg[None, :])
    by_head = block_cum.T
    spread = by_head[:, :, None] - by_head[:, None, :]
    decay_table = jnp.where(allowed[None], jnp.exp(jnp.where(allowed[None], spread, 0.0)), 0.0)
    scores = jnp.einsum("thd,shd->hts", block_q, block_k, preferred_element_type=jnp.float32)
    inside = paired_einsum("hts,shd->thd", scores * decay_table, block_v, True)
    end_seg = block_seg[-1]
    toward = jnp.where(
        (block_seg == end_seg)[:, None], jnp.exp(block_cum[-1][None, :] - block_cum), 0.0
    )
    local_state = paired_einsum(
        "shd,she->hde", block_k.astype(jnp.float32) * toward[:, :, None], block_v, True
    )
    keep_factor = jnp.where(jnp.all(linked), jnp.exp(block_cum[-1]), 0.0)
    new_state = keep_factor[:, None, None] * run_state + local_state
    return (earlier + inside, new_state)


def attend(own_q, own_k, own_v, cumulative, segment, run_state, last_seg):
    block_out, run_state = block_terms(
        run_state, last_seg, own_q, own_k, own_v, cumulative, segment
    )
    return (block_out, run_state)


def carried_state(factor, end_state):
    owner_count = lax.axis_size("ctx")
    my_index = lax.axis_index("ctx")
    factors, states = (
        lax.all_gather(factor[None].astype(jnp.bfloat16), "ctx", axis=0, tiled=True).astype(
            jnp.float32
        ),
        lax.all_gather(end_state[None].astype(jnp.bfloat16), "ctx", axis=0, tiled=True).astype(
            jnp.float32
        ),
    )
    index_line = jnp.arange(owner_count)
    between = (index_line[None, :] > index_line[:, None]) & (index_line[None, :] < my_index)
    chain_weights = jnp.prod(jnp.where(between[:, :, None], factors[None, :, :], 1.0), axis=1)
    chain_weights = chain_weights * (index_line < my_index)[:, None].astype(jnp.float32)
    return jnp.einsum("nh,nhde->hde", chain_weights, states, precision=lax.Precision.HIGHEST)


def local_by_rows(
    queries, keys, values, log_decay, arrival_positions, prompt_lengths, norm_gain, out_weight
):
    row_count = queries.shape[0]
    heads_here = log_decay.shape[1]
    head_width = queries.shape[1] // heads_here
    owner_count = lax.axis_size("ctx")
    my_index = lax.axis_index("ctx")
    capacity = 3 * (row_count // (2 * owner_count))
    slot_total = owner_count * capacity
    every_position = lax.all_gather(arrival_positions, "ctx", axis=0, tiled=True)
    target = arrival_positions // row_count
    hit_table = (target[:, None] == jnp.arange(owner_count)[None, :]).astype(jnp.int32)
    slot_index = jnp.sum((jnp.cumsum(hit_table, axis=0) - 1) * hit_table, axis=1)
    send_slot = target * capacity + slot_index
    send_onehot = (jnp.arange(slot_total)[:, None] == send_slot[None, :]).astype(jnp.bfloat16)

    def pack_rows(source):
        packed = jnp.dot(send_onehot, source, preferred_element_type=jnp.float32).astype(
            source.dtype
        )
        return packed.reshape(owner_count, capacity, source.shape[1])

    arrived = (
        lax.all_to_all(pack_rows(queries), "ctx", split_axis=0, concat_axis=0, tiled=True),
        lax.all_to_all(pack_rows(keys), "ctx", split_axis=0, concat_axis=0, tiled=True),
        lax.all_to_all(pack_rows(values), "ctx", split_axis=0, concat_axis=0, tiled=True),
        lax.all_to_all(pack_rows(log_decay), "ctx", split_axis=0, concat_axis=0, tiled=True),
    )
    layout = every_position.reshape(owner_count, row_count)
    own_rows = layout // row_count == my_index
    rank_index = jnp.cumsum(own_rows.astype(jnp.int32), axis=1) - 1
    source_slot = (jnp.arange(owner_count)[:, None] * capacity + rank_index).reshape(-1)
    wanted = my_index * row_count + jnp.arange(row_count, dtype=jnp.int32)
    matches = every_position[None, :] == wanted[:, None]
    slot_of_row = jnp.sum(jnp.where(matches, source_slot[None, :], 0), axis=1)
    receive_onehot = (slot_of_row[:, None] == jnp.arange(slot_total)[None, :]).astype(jnp.bfloat16)

    def unpack_rows(buffer):
        flat_buffer = buffer.reshape(slot_total, buffer.shape[2])
        return jnp.dot(receive_onehot, flat_buffer, preferred_element_type=jnp.float32).astype(
            buffer.dtype
        )

    own_q = unpack_rows(arrived[0]).reshape(row_count, heads_here, head_width)
    own_k = unpack_rows(arrived[1]).reshape(row_count, heads_here, head_width)
    own_v = unpack_rows(arrived[2]).reshape(row_count, heads_here, head_width)
    cumulative = jnp.cumsum(unpack_rows(arrived[3]).astype(jnp.float32), axis=0)
    positions = my_index * row_count + jnp.arange(row_count, dtype=jnp.int32)
    prompt_ends = jnp.cumsum(prompt_lengths)[:-1]
    segment = jnp.sum((positions[:, None] >= prompt_ends[None, :]).astype(jnp.int32), axis=1)
    opens_prompt = (positions[0] == 0) | jnp.any(positions[0] == prompt_ends)
    through = jnp.logical_not(opens_prompt) & jnp.all(segment == segment[0])
    factor = jnp.where(through, jnp.exp(cumulative[-1]), 0.0)
    entry_seg = jnp.where(opens_prompt, -1, segment[0])
    empty_state = jnp.zeros((heads_here, head_width, head_width), jnp.float32)
    attention, end_state = attend(
        own_q, own_k, own_v, cumulative, segment, empty_state, jnp.int32(-1)
    )
    incoming = carried_state(factor, end_state)
    reach_back = jnp.where((segment == entry_seg)[:, None], jnp.exp(cumulative), 0.0)
    attention = (
        attention + paired_einsum("thd,hde->the", incoming, own_q, False) * reach_back[:, :, None]
    )
    inv_scale = lax.rsqrt(jnp.mean(attention * attention, axis=-1, keepdims=True) + 1e-06)
    normed = (attention * inv_scale * norm_gain.reshape(heads_here, head_width)).astype(
        jnp.bfloat16
    )
    normed = normed.reshape(row_count, heads_here * head_width)
    projected = jnp.dot(
        lax.all_gather(normed, "head", axis=1, tiled=True),
        out_weight,
        preferred_element_type=jnp.float32,
    )
    return projected.astype(jnp.bfloat16)


def local(
    queries, keys, values, log_decay, arrival_positions, prompt_lengths, norm_gain, out_weight
):
    heads, owners = log_decay.shape[1], lax.axis_size("ctx")
    head_width = queries.shape[1] // heads
    fits = heads % owners == 0 and head_width == LANES and queries.shape[0] % LANES == 0
    plan = local_by_heads if fits and heads < META else local_by_rows
    return plan(
        queries, keys, values, log_decay, arrival_positions, prompt_lengths, norm_gain, out_weight
    )


def solution(mesh):
    return jax.shard_map(
        local,
        mesh=mesh,
        in_specs=(
            P(("groups", "ctx"), "head"),
            P(("groups", "ctx"), "head"),
            P(("groups", "ctx"), "head"),
            P(("groups", "ctx"), "head"),
            P(("groups", "ctx")),
            P("groups"),
            P("head"),
            P(None, "head"),
        ),
        out_specs=P(("groups", "ctx"), "head"),
        check_vma=False,
    )
```

```python
import functools
import math

import jax
import jax.numpy as jnp
from jax import lax
from jax.experimental import pallas as pl
from jax.experimental.pallas import tpu as pltpu
from jax.sharding import PartitionSpec as P


LANES = 128
AUX = 16
CUT = -256.0
MIB = 1024 * 1024
AHEAD = 1
SMEM = pl.BlockSpec(memory_space=pltpu.SMEM)
VMEM = pl.BlockSpec(memory_space=pltpu.VMEM)
HBM = pl.BlockSpec(memory_space=pltpu.HBM)
ANY = pl.BlockSpec(memory_space=pl.ANY)
NN = ((1,), (0,))
NT = ((1,), (1,))


def grant(mib):
    return pltpu.CompilerParams(vmem_limit_bytes=mib * MIB)


def mxu(a, b, dims=NN):
    return lax.dot_general(a, b, (dims, ((), ())), preferred_element_type=jnp.float32)


def iota(shape, dim):
    return lax.broadcasted_iota(jnp.int32, shape, dim)


def whole(values):
    return values.astype(jnp.int32).astype(jnp.float32)


def tile_of(n):
    return slice(n * LANES, (n + 1) * LANES)


def layout(owners, pos_ref, decay_ref, lengths_ref):
    heads, rows = decay_ref.shape
    unit = rows // (2 * owners)
    pos_row = pos_ref[...].astype(jnp.float32)
    pos_col = jnp.transpose(jnp.broadcast_to(pos_row, (LANES, rows)))[:, 0:1]
    rank = jnp.sum((pos_col < pos_row).astype(jnp.float32), axis=0, keepdims=True)
    order = (iota((rows, rows), 0).astype(jnp.float32) == rank).astype(jnp.bfloat16)
    spare = jnp.zeros((AUX - 1 - heads, rows), jnp.float32)
    aux = jnp.concatenate(
        [decay_ref[...].astype(jnp.float32), spare, whole(pos_row * (1.0 / unit))], axis=0
    ).astype(jnp.bfloat16)
    by_row = mxu(aux, order, NT)
    by_col = mxu(order, aux, NT)
    units = by_row[AUX - 1 : AUX, :]
    per_owner = 1.0 / (rows // unit)
    owner_row, owner_col = whole(units * per_owner), whole(by_col[:, AUX - 1 : AUX] * per_owner)
    place = units.astype(jnp.int32) * unit + lax.rem(iota((1, rows), 1), unit)
    decay = by_row
    end = 0
    for j in range(lengths_ref.shape[0] - 1):
        end = end + lengths_ref[j]
        decay = jnp.where(place == end, CUT, decay)
    return order, decay.astype(jnp.bfloat16), units, owner_row, owner_col


def half_copies(sources, targets, sems, span):
    copies = [
        pltpu.make_async_copy(source.at[:, span], target, sems.at[n])
        for n, (source, target) in enumerate(zip(sources, targets))
    ]
    for copy in copies:
        copy.start()
    return copies


def states_kernel(owners, half, me_ref, pos_ref, decay_ref, lengths_ref, k_hbm, v_hbm, *refs):
    outs, (k_in, v_in, held, sems) = refs[:owners], refs[owners:]
    rows, width = k_in.shape
    copies = half_copies((k_hbm, v_hbm), (k_in, v_in), sems, pl.ds(half * width, width))
    order, decay, units, owner_row, owner_col = layout(owners, pos_ref, decay_ref, lengths_ref)
    after = (iota((rows, rows), 0) > iota((rows, rows), 1)) & (owner_col == owner_row)
    toward = jnp.exp(mxu(decay, after.astype(jnp.bfloat16)))
    of_owner = [owner_row == float(o) for o in range(owners)]
    line = iota((4 * owners, LANES), 0)
    marks = jnp.zeros((4 * owners, LANES), jnp.float32)
    sums = []
    for o in range(owners):
        first = jnp.min(jnp.where(of_owner[o], units, 1e9), axis=1, keepdims=True)
        marks = jnp.where(line == 3 * owners + o, first, marks)
        rest = jnp.sum(
            jnp.where(of_owner[o], decay.astype(jnp.float32), 0.0), axis=1, keepdims=True
        )
        for part in range(3):
            short = rest.astype(jnp.bfloat16).astype(jnp.float32)
            sums.append((part * owners + o, short))
            rest = rest - short
    copies[0].wait()
    turned = jnp.transpose(mxu(order, k_in[...]))
    copies[1].wait()
    v = mxu(order, v_in[...]).astype(jnp.bfloat16)
    for n in range(owners):
        h = half * owners + n
        k = turned[tile_of(n), :] * toward[h : h + 1, :]
        split = jnp.concatenate([jnp.where(own, k, 0.0) for own in of_owner], axis=0)
        held[n, :width, :] = mxu(split.astype(jnp.bfloat16), v[:, tile_of(n)]).astype(
            jnp.bfloat16
        )
        block = marks
        for at, short in sums:
            block = jnp.where(line == at, short[h : h + 1, :], block)
        held[n, width:, :] = block.astype(jnp.bfloat16)
    for s in range(owners):
        outs[s][...] = held[lax.rem(me_ref[0] + s, owners)]


def states(owners, half, me, positions, decays, lengths, keys, values):
    rows = keys.shape[0]
    width = owners * LANES
    out = jax.ShapeDtypeStruct((width + 4 * owners, LANES), jnp.bfloat16)
    return pl.pallas_call(
        functools.partial(states_kernel, owners, half),
        out_shape=[out] * owners,
        in_specs=[SMEM, VMEM, VMEM, SMEM, HBM, HBM],
        out_specs=[VMEM] * owners,
        scratch_shapes=[
            pltpu.VMEM((rows, width), jnp.bfloat16),
            pltpu.VMEM((rows, width), jnp.bfloat16),
            pltpu.VMEM((owners, *out.shape), jnp.bfloat16),
            pltpu.SemaphoreType.DMA((2,)),
        ],
        compiler_params=grant(60),
        cost_estimate=pl.CostEstimate(flops=6 * rows * rows * width, bytes_accessed=rows * width * 6, transcendentals=0),
        name="run_states",
    )(me, positions, decays, lengths, keys, values)


def inside_kernel(owners, half, pos_ref, decay_ref, lengths_ref, q_hbm, k_hbm, v_hbm, *refs):
    q_out, out, q_in, k_in, v_in, sems = refs
    rows, width = q_in.shape
    span = pl.ds(half * width, width)
    copies = half_copies((q_hbm, k_hbm, v_hbm), (q_in, k_in, v_in), sems, span)
    order, decay, _, owner_row, owner_col = layout(owners, pos_ref, decay_ref, lengths_ref)
    seen = (iota((rows, rows), 0) >= iota((rows, rows), 1)) & (owner_col == owner_row)
    counted = seen.astype(jnp.bfloat16)
    total_row, total_col = mxu(decay, counted, NT), mxu(counted, decay, NT)
    reach = jnp.exp(total_col)
    band = -(-(3 * rows // (2 * owners)) // LANES) * LANES
    for copy in copies:
        copy.wait()
    for source in (q_in, k_in, v_in):
        source[...] = mxu(order, source[...]).astype(jnp.bfloat16)
    for n in range(owners):
        h = half * owners + n
        cols = tile_of(n)
        q_out[:, cols] = (q_in[:, cols].astype(jnp.float32) * reach[:, h : h + 1]).astype(
            jnp.bfloat16
        )
        for top in range(0, rows, LANES):
            here = slice(top, top + LANES)
            past = slice(max(0, top - band), top + LANES)
            gap = total_col[here, h : h + 1] - total_row[h : h + 1, past]
            table = jnp.exp(jnp.where(seen[here, past], gap, -1e30))
            scores = mxu(q_in[here, cols], k_in[past, cols], NT) * table
            out[here, cols] = mxu(scores.astype(jnp.bfloat16), v_in[past, cols])


def inside(owners, half, positions, decays, lengths, queries, keys, values):
    rows = queries.shape[0]
    shape = (rows, owners * LANES)
    return pl.pallas_call(
        functools.partial(inside_kernel, owners, half),
        out_shape=[
            jax.ShapeDtypeStruct(shape, jnp.bfloat16),
            jax.ShapeDtypeStruct(shape, jnp.float32),
        ],
        in_specs=[VMEM, VMEM, SMEM, HBM, HBM, HBM],
        out_specs=[VMEM, VMEM],
        scratch_shapes=[pltpu.VMEM(shape, jnp.bfloat16)] * 3 + [pltpu.SemaphoreType.DMA((3,))],
        compiler_params=grant(24),
        cost_estimate=pl.CostEstimate(flops=6 * rows * rows * shape[1], bytes_accessed=rows * shape[1] * 12, transcendentals=owners * rows * rows),
        name="attend_inside_runs",
    )(positions, decays, lengths, queries, keys, values)


def chain_kernel(owners, *refs):
    blocks, outs = refs[:owners], refs[owners:]
    size = owners * LANES + 4 * owners
    for half in range(blocks[0].shape[0] // size):
        base = half * size
        marks = [b[base + owners * LANES : base + size, :].astype(jnp.float32) for b in blocks]
        state = jnp.zeros((LANES, LANES), jnp.float32)
        for o in range(owners):
            starts = [m[3 * owners + o : 3 * owners + o + 1, :] for m in marks]
            keeps = [
                jnp.exp(sum(m[p * owners + o : p * owners + o + 1, :] for p in range(3)))
                for m in marks
            ]
            ranks = [sum((other < own).astype(jnp.float32) for other in starts) for own in starts]
            runs = [b[base + o * LANES : base + (o + 1) * LANES, :] for b in blocks]
            before = []
            for place in range(owners):
                run, keep = runs[-1], keeps[-1]
                for s in range(owners - 1):
                    chosen = ranks[s] == float(place)
                    run = jnp.where(chosen, runs[s], run)
                    keep = jnp.where(chosen, keeps[s], keep)
                before.append(state.astype(jnp.bfloat16))
                state = keep * state + run.astype(jnp.float32)
            for s in range(owners):
                entry = before[-1]
                for place in range(owners - 1):
                    entry = jnp.where(ranks[s] == float(place), before[place], entry)
                row = half * owners * LANES + o * LANES
                outs[s][row : row + LANES, :] = entry


def chain(owners, blocks):
    size = owners * LANES + 4 * owners
    rows = blocks[0].shape[0] // size * owners * LANES
    return pl.pallas_call(
        functools.partial(chain_kernel, owners),
        out_shape=[jax.ShapeDtypeStruct((rows, LANES), jnp.bfloat16)] * owners,
        in_specs=[VMEM] * owners,
        out_specs=[VMEM] * owners,
        compiler_params=grant(12),
        cost_estimate=pl.CostEstimate(flops=owners * rows * LANES * 8, bytes_accessed=owners * rows * LANES * 4, transcendentals=0),
        name="chain_states",
    )(*blocks)


def finish_kernel(owners, me_ref, bounds_ref, gain_ref, q_ref, inside_ref, *refs):
    entries, outs, (held, normed) = refs[:owners], refs[owners:-2], refs[-2:]
    rows = q_ref.shape[0]
    unit = rows // (2 * owners)
    for s in range(owners):
        held[lax.rem(me_ref[0] + s, owners)] = entries[s][...]
    row = iota((rows, LANES), 0)
    mine = []
    for o in range(owners):
        top = bounds_ref[o + 1] if o + 1 < owners else rows
        mine.append((row >= bounds_ref[o]) & (row < top))
    for h in range(owners):
        q = q_ref[:, tile_of(h)]
        spread = jnp.concatenate([jnp.where(own, q, jnp.zeros_like(q)) for own in mine], axis=1)
        out = inside_ref[:, tile_of(h)] + mxu(spread, held[h])
        scale = lax.rsqrt(jnp.mean(out * out, axis=1, keepdims=True) + 1e-06)
        normed[:rows, tile_of(h)] = (out * scale * gain_ref[:, tile_of(h)]).astype(jnp.bfloat16)
    normed[rows:, :] = jnp.zeros((normed.shape[0] - rows, normed.shape[1]), jnp.bfloat16)
    for s in range(owners):
        start = pl.multiple_of(bounds_ref[lax.rem(me_ref[0] + s, owners)], unit)
        outs[s][...] = normed[pl.ds(start, 3 * unit), :]


def finish(owners, me, bounds, gain, scaled, within, entries):
    rows, width = scaled.shape
    unit = rows // (2 * owners)
    out = jax.ShapeDtypeStruct((3 * unit, width), jnp.bfloat16)
    return pl.pallas_call(
        functools.partial(finish_kernel, owners),
        out_shape=[out] * owners,
        in_specs=[SMEM, SMEM] + [VMEM] * (3 + owners),
        out_specs=[VMEM] * owners,
        scratch_shapes=[
            pltpu.VMEM((owners, owners * LANES, LANES), jnp.bfloat16),
            pltpu.VMEM((rows + 2 * unit, width), jnp.bfloat16),
        ],
        compiler_params=grant(20),
        cost_estimate=pl.CostEstimate(flops=2 * rows * width * width, bytes_accessed=rows * width * 10, transcendentals=0),
        name="finish_heads",
    )(me, bounds, gain, scaled, within, *entries)


def gather_kernel(owners, me_ref, starts_ref, *refs):
    runs, out = refs[:owners], refs[-1]
    unit = runs[0].shape[0] // 3
    per_owner = out.shape[0] // unit
    firsts = [starts_ref[s * owners + me_ref[0]] - me_ref[0] * per_owner for s in range(owners)]
    for s in range(owners):
        after = jnp.int32(per_owner)
        for other in firsts:
            after = jnp.where((other > firsts[s]) & (other < after), other, after)
        out[pl.ds(pl.multiple_of(firsts[s] * unit, unit), unit), :] = runs[s][:unit, :]

        @pl.when(after - firsts[s] > 1)
        def _(s=s):
            to = pl.multiple_of((firsts[s] + 1) * unit, unit)
            out[pl.ds(to, 2 * unit), :] = runs[s][unit:, :]


def gather_rows(owners, rows, me, starts, runs, tokens):
    width = runs[0].shape[1]
    return pl.pallas_call(
        functools.partial(gather_kernel, owners),
        out_shape=jax.ShapeDtypeStruct((rows, width), jnp.bfloat16),
        in_specs=[SMEM, SMEM] + [VMEM] * owners + [ANY] * len(tokens),
        out_specs=VMEM,
        compiler_params=grant(8),
        cost_estimate=pl.CostEstimate(flops=0, bytes_accessed=rows * width * 5, transcendentals=0),
        name="gather_own_rows",
    )(me, starts, *runs, *tokens)


def weight_rows(mine_ref, weight, places, depths):
    rows = []
    for (flip, first), depth in zip(places, depths):
        top = (mine_ref[0] ^ flip) * mine_ref[1] + first * LANES
        rows.append(weight.at[pl.ds(pl.multiple_of(top, LANES), depth), :])
    return rows


def fetch_rows(mine_ref, weight, places, depths, stacked, sems):
    at = 0
    copies = []
    for n, rows in enumerate(weight_rows(mine_ref, weight, places, depths)):
        copies.append(
            pltpu.make_async_copy(rows, stacked.at[pl.ds(at, depths[n]), :], sems.at[n])
        )
        copies[-1].start()
        at += depths[n]
    return copies


def hold_kernel(places, depths, mine_ref, weight, out, token, sems):
    token[...] = jnp.zeros_like(token)
    for copy in fetch_rows(mine_ref, weight, places, depths, out, sems):
        copy.wait()


def hold_rows(mine, weight, places, depths):
    return pl.pallas_call(
        functools.partial(hold_kernel, places, depths),
        out_shape=[
            pltpu.VMEM((sum(depths), weight.shape[1]), weight.dtype),
            jax.ShapeDtypeStruct((8, LANES), jnp.float32),
        ],
        in_specs=[SMEM, HBM],
        out_specs=[VMEM, VMEM],
        scratch_shapes=[pltpu.SemaphoreType.DMA((len(places),))],
        compiler_params=grant(4),
        name="hold_weight",
    )(mine, pltpu.with_memory_space_constraint(weight, pltpu.HBM))


def project_kernel(places, carried, mine_ref, *refs):
    count = len(places)
    parts, weight, rest = refs[:count], refs[count], refs[count + 1 :]
    out, token, stacked, sems = rest[-4:]
    depths = [part.shape[1] for part in parts]
    token[...] = jnp.zeros_like(token)
    for copy in fetch_rows(mine_ref, weight, places, depths, stacked, sems):
        copy.wait()
    rows = out.shape[0]
    tile = math.gcd(rows, LANES)
    for n in range(rows // tile):
        span = slice(n * tile, (n + 1) * tile)
        total = rest[0][span, :] if carried else None
        at = 0
        for part in parts:
            depth = part.shape[1]
            term = mxu(part[span, :], stacked[at : at + depth, :])
            total = term if total is None else total + term
            at += depth
        out[span, :] = total


def project(mine, places, parts, weight, carried):
    rows, width = parts[0].shape[0], weight.shape[1]
    depth = sum(part.shape[1] for part in parts)
    extra = [] if carried is None else [pltpu.with_memory_space_constraint(carried, pltpu.VMEM)]
    return pl.pallas_call(
        functools.partial(project_kernel, places, carried is not None),
        out_shape=[
            pltpu.VMEM((rows, width), jnp.float32),
            jax.ShapeDtypeStruct((8, LANES), jnp.float32),
        ],
        in_specs=[SMEM] + [VMEM] * len(parts) + [HBM] + [VMEM] * len(extra),
        out_specs=[VMEM, VMEM],
        scratch_shapes=[
            pltpu.VMEM((depth, width), jnp.bfloat16),
            pltpu.SemaphoreType.DMA((len(parts),)),
        ],
        compiler_params=grant(20),
        name="project",
    )(mine, *parts, pltpu.with_memory_space_constraint(weight, pltpu.HBM), *extra)


def project_last_kernel(count, *refs):
    parts, (held, carried, _, out, tiles, sems) = refs[:count], refs[count:]
    rows = tiles.shape[0]
    tile = math.gcd(rows, LANES)
    stores = []
    for n in range(rows // tile):
        span = slice(n * tile, (n + 1) * tile)
        total = carried[span, :]
        at = 0
        for part in parts:
            depth = part.shape[1]
            total = total + mxu(part[span, :], held[at : at + depth, :])
            at += depth
        tiles[span, :] = total.astype(tiles.dtype)
        stores.append(
            pltpu.make_async_copy(tiles.at[span, :], out.at[span, :], sems.at[n])
        )
        stores[-1].start()
    for store in stores:
        store.wait()


def project_last(parts, held, carried, token):
    rows, width = carried.shape
    held, carried = (
        pltpu.with_memory_space_constraint(x, pltpu.VMEM) for x in (held, carried)
    )
    return pl.pallas_call(
        functools.partial(project_last_kernel, len(parts)),
        out_shape=pltpu.HBM((rows, width), jnp.bfloat16),
        in_specs=[VMEM] * (len(parts) + 2) + [ANY],
        out_specs=HBM,
        scratch_shapes=[
            pltpu.VMEM((rows, width), jnp.bfloat16),
            pltpu.SemaphoreType.DMA((rows // math.gcd(rows, LANES),)),
        ],
        compiler_params=grant(8),
        name="project_last",
    )(*parts, held, carried, token)


def shift_pairs(count, shift):
    return [(a, (a + shift) % count) for a in range(count)]


def exchange(owners, blocks, way):
    return [blocks[0]] + [
        lax.ppermute(blocks[s], "ctx", shift_pairs(owners, way * s)) for s in range(1, owners)
    ]


def local_by_runs(
    queries, keys, values, log_decay, arrival_positions, prompt_lengths, norm_gain, out_weight
):
    rows, width = queries.shape
    heads = log_decay.shape[1]
    owners = lax.axis_size("ctx")
    columns = lax.axis_size("head")
    mine = lax.axis_index("head")
    me = lax.axis_index("ctx").astype(jnp.int32).reshape(1)
    positions, decays = arrival_positions[None, :], log_decay.T
    halves = heads // owners
    depth = owners * LANES
    queries, keys, values = (
        pltpu.with_memory_space_constraint(x, pltpu.HBM) for x in (queries, keys, values)
    )
    gain = norm_gain.reshape(halves, 1, depth)
    blocks = []
    for half in range(halves):
        sent = states(owners, half, me, positions, decays, prompt_lengths, keys, values)
        blocks.append(exchange(owners, sent, 1))
    within = [
        inside(owners, half, positions, decays, prompt_lengths, queries, keys, values)
        for half in range(halves)
    ]
    blocks[0], within = lax.optimization_barrier((blocks[0], within))
    lines = rows * jnp.arange(owners, dtype=jnp.int32)
    bounds = jnp.sum((arrival_positions[:, None] < lines[None, :]).astype(jnp.int32), axis=0)
    first_mark = depth + 3 * owners
    starts = jnp.concatenate([b[first_mark : first_mark + owners, 0] for b in blocks[0]])
    starts = starts.astype(jnp.int32)
    entries = []
    for half in range(halves):
        linked = chain(owners, blocks[half])
        entries.append(exchange(owners, linked, -1))

    def flip_head(part, flip):
        return lax.ppermute(part, "head", [(a, a ^ flip) for a in range(columns)])

    runs = []
    for half in range(halves):
        sent = finish(owners, me, bounds, gain[half], *within[half], entries[half])
        runs.append(exchange(owners, sent, 1))
    scalars = jnp.stack([mine, width]).astype(jnp.int32)
    far_columns = range(2, columns, 2)
    group, total, tokens = [], None, []
    crossed = []
    for half in range(halves):
        first = half * owners
        last = half == halves - 1
        if not last:
            runs[half], runs[half + 1][1] = lax.optimization_barrier(
                (runs[half], runs[half + 1][1])
            )
        elif group:
            total, token = project(
                scalars, [at for at, _ in group], [part for _, part in group], out_weight, None
            )
            tokens.append(token)
            group = []
        if last:
            late = [(flip, first) for far in far_columns for flip in (far, far + 1)]
            held, token = hold_rows(scalars, out_weight, late, [depth] * len(late))
            tokens.append(token)
        normed = gather_rows(owners, rows, me, starts, runs[half], tokens)
        if last:
            moved, normed = lax.optimization_barrier(([part for _, _, part in crossed], normed))
            crossed = [(far, at, part) for (far, at, _), part in zip(crossed, moved)]
        group += [((0, first), normed), ((1, first), flip_head(normed, 1))]
        across = [flip_head(normed, far) for far in far_columns]
        if last:
            for far, at, part in crossed:
                group += [((far, at), part), ((far + 1, at), flip_head(part, 1))]
            total, token = project(
                scalars, [at for at, _ in group], [part for _, part in group], out_weight, total
            )
            across[0], token = lax.optimization_barrier((across[0], token))
            group = []
            for far, part in zip(far_columns, across):
                group += [((far, first), part), ((far + 1, first), flip_head(part, 1))]
        else:
            crossed += [(far, first, part) for far, part in zip(far_columns, across)]
    return project_last([part for _, part in group], held, total, token)


def split_terms(source):
    upper_part = source.astype(jnp.bfloat16)
    lower_part = (source - upper_part.astype(jnp.float32)).astype(jnp.bfloat16)
    return (upper_part, lower_part)


def paired_einsum(form, wide_operand, narrow_operand, wide_first):
    upper_part, lower_part = split_terms(wide_operand)
    if wide_first:
        return jnp.einsum(
            form, upper_part, narrow_operand, preferred_element_type=jnp.float32
        ) + jnp.einsum(form, lower_part, narrow_operand, preferred_element_type=jnp.float32)
    return jnp.einsum(
        form, narrow_operand, upper_part, preferred_element_type=jnp.float32
    ) + jnp.einsum(form, narrow_operand, lower_part, preferred_element_type=jnp.float32)


def block_terms(run_state, last_seg, block_q, block_k, block_v, block_cum, block_seg):
    linked = block_seg == last_seg
    reach_back = jnp.where(linked[:, None], jnp.exp(block_cum), 0.0)
    earlier = paired_einsum("thd,hde->the", run_state, block_q, False) * reach_back[:, :, None]
    block_rows = block_seg.shape[0]
    order_ok = jnp.arange(block_rows)[:, None] >= jnp.arange(block_rows)[None, :]
    allowed = order_ok & (block_seg[:, None] == block_seg[None, :])
    by_head = block_cum.T
    spread = by_head[:, :, None] - by_head[:, None, :]
    decay_table = jnp.where(allowed[None], jnp.exp(jnp.where(allowed[None], spread, 0.0)), 0.0)
    scores = jnp.einsum("thd,shd->hts", block_q, block_k, preferred_element_type=jnp.float32)
    inside = paired_einsum("hts,shd->thd", scores * decay_table, block_v, True)
    end_seg = block_seg[-1]
    toward = jnp.where(
        (block_seg == end_seg)[:, None], jnp.exp(block_cum[-1][None, :] - block_cum), 0.0
    )
    local_state = paired_einsum(
        "shd,she->hde", block_k.astype(jnp.float32) * toward[:, :, None], block_v, True
    )
    keep_factor = jnp.where(jnp.all(linked), jnp.exp(block_cum[-1]), 0.0)
    new_state = keep_factor[:, None, None] * run_state + local_state
    return (earlier + inside, new_state)


def attend(own_q, own_k, own_v, cumulative, segment, run_state, last_seg):
    block_out, run_state = block_terms(
        run_state, last_seg, own_q, own_k, own_v, cumulative, segment
    )
    return (block_out, run_state)


def carried_state(factor, end_state):
    owner_count = lax.axis_size("ctx")
    my_index = lax.axis_index("ctx")
    factors, states = (
        lax.all_gather(factor[None].astype(jnp.bfloat16), "ctx", axis=0, tiled=True).astype(
            jnp.float32
        ),
        lax.all_gather(end_state[None].astype(jnp.bfloat16), "ctx", axis=0, tiled=True).astype(
            jnp.float32
        ),
    )
    index_line = jnp.arange(owner_count)
    between = (index_line[None, :] > index_line[:, None]) & (index_line[None, :] < my_index)
    chain_weights = jnp.prod(jnp.where(between[:, :, None], factors[None, :, :], 1.0), axis=1)
    chain_weights = chain_weights * (index_line < my_index)[:, None].astype(jnp.float32)
    return jnp.einsum("nh,nhde->hde", chain_weights, states, precision=lax.Precision.HIGHEST)


def local_by_rows(
    queries, keys, values, log_decay, arrival_positions, prompt_lengths, norm_gain, out_weight
):
    row_count = queries.shape[0]
    heads_here = log_decay.shape[1]
    head_width = queries.shape[1] // heads_here
    owner_count = lax.axis_size("ctx")
    my_index = lax.axis_index("ctx")
    capacity = 3 * (row_count // (2 * owner_count))
    slot_total = owner_count * capacity
    every_position = lax.all_gather(arrival_positions, "ctx", axis=0, tiled=True)
    target = arrival_positions // row_count
    hit_table = (target[:, None] == jnp.arange(owner_count)[None, :]).astype(jnp.int32)
    slot_index = jnp.sum((jnp.cumsum(hit_table, axis=0) - 1) * hit_table, axis=1)
    send_slot = target * capacity + slot_index
    send_onehot = (jnp.arange(slot_total)[:, None] == send_slot[None, :]).astype(jnp.bfloat16)

    def pack_rows(source):
        packed = jnp.dot(send_onehot, source, preferred_element_type=jnp.float32).astype(
            source.dtype
        )
        return packed.reshape(owner_count, capacity, source.shape[1])

    arrived = (
        lax.all_to_all(pack_rows(queries), "ctx", split_axis=0, concat_axis=0, tiled=True),
        lax.all_to_all(pack_rows(keys), "ctx", split_axis=0, concat_axis=0, tiled=True),
        lax.all_to_all(pack_rows(values), "ctx", split_axis=0, concat_axis=0, tiled=True),
        lax.all_to_all(pack_rows(log_decay), "ctx", split_axis=0, concat_axis=0, tiled=True),
    )
    layout = every_position.reshape(owner_count, row_count)
    own_rows = layout // row_count == my_index
    rank_index = jnp.cumsum(own_rows.astype(jnp.int32), axis=1) - 1
    source_slot = (jnp.arange(owner_count)[:, None] * capacity + rank_index).reshape(-1)
    wanted = my_index * row_count + jnp.arange(row_count, dtype=jnp.int32)
    matches = every_position[None, :] == wanted[:, None]
    slot_of_row = jnp.sum(jnp.where(matches, source_slot[None, :], 0), axis=1)
    receive_onehot = (slot_of_row[:, None] == jnp.arange(slot_total)[None, :]).astype(jnp.bfloat16)

    def unpack_rows(buffer):
        flat_buffer = buffer.reshape(slot_total, buffer.shape[2])
        return jnp.dot(receive_onehot, flat_buffer, preferred_element_type=jnp.float32).astype(
            buffer.dtype
        )

    own_q = unpack_rows(arrived[0]).reshape(row_count, heads_here, head_width)
    own_k = unpack_rows(arrived[1]).reshape(row_count, heads_here, head_width)
    own_v = unpack_rows(arrived[2]).reshape(row_count, heads_here, head_width)
    cumulative = jnp.cumsum(unpack_rows(arrived[3]).astype(jnp.float32), axis=0)
    positions = my_index * row_count + jnp.arange(row_count, dtype=jnp.int32)
    prompt_ends = jnp.cumsum(prompt_lengths)[:-1]
    segment = jnp.sum((positions[:, None] >= prompt_ends[None, :]).astype(jnp.int32), axis=1)
    opens_prompt = (positions[0] == 0) | jnp.any(positions[0] == prompt_ends)
    through = jnp.logical_not(opens_prompt) & jnp.all(segment == segment[0])
    factor = jnp.where(through, jnp.exp(cumulative[-1]), 0.0)
    entry_seg = jnp.where(opens_prompt, -1, segment[0])
    empty_state = jnp.zeros((heads_here, head_width, head_width), jnp.float32)
    attention, end_state = attend(
        own_q, own_k, own_v, cumulative, segment, empty_state, jnp.int32(-1)
    )
    incoming = carried_state(factor, end_state)
    reach_back = jnp.where((segment == entry_seg)[:, None], jnp.exp(cumulative), 0.0)
    attention = (
        attention + paired_einsum("thd,hde->the", incoming, own_q, False) * reach_back[:, :, None]
    )
    inv_scale = lax.rsqrt(jnp.mean(attention * attention, axis=-1, keepdims=True) + 1e-06)
    normed = (attention * inv_scale * norm_gain.reshape(heads_here, head_width)).astype(
        jnp.bfloat16
    )
    normed = normed.reshape(row_count, heads_here * head_width)
    projected = jnp.dot(
        lax.all_gather(normed, "head", axis=1, tiled=True),
        out_weight,
        preferred_element_type=jnp.float32,
    )
    return projected.astype(jnp.bfloat16)


def local(
    queries, keys, values, log_decay, arrival_positions, prompt_lengths, norm_gain, out_weight
):
    heads, owners = log_decay.shape[1], lax.axis_size("ctx")
    head_width = queries.shape[1] // heads
    unit = queries.shape[0] // (2 * owners)
    fits = heads % owners == 0 and heads < AUX and head_width == LANES
    fits = fits and queries.shape[0] % LANES == 0 and unit % 16 == 0 and owners % 4 == 0
    plan = local_by_runs if fits else local_by_rows
    return plan(
        queries, keys, values, log_decay, arrival_positions, prompt_lengths, norm_gain, out_weight
    )


def solution(mesh):
    return jax.shard_map(
        local,
        mesh=mesh,
        in_specs=(
            P(("groups", "ctx"), "head"),
            P(("groups", "ctx"), "head"),
            P(("groups", "ctx"), "head"),
            P(("groups", "ctx"), "head"),
            P(("groups", "ctx")),
            P("groups"),
            P("head"),
            P(None, "head"),
        ),
        out_specs=P(("groups", "ctx"), "head"),
        check_vma=False,
    )
```

```python
import functools
import math

import jax
import jax.numpy as jnp
from jax import lax
from jax.experimental import pallas as pl
from jax.experimental.pallas import tpu as pltpu
from jax.sharding import PartitionSpec as P


LANES = 128
AUX = 16
CUT = -256.0
MIB = 1024 * 1024
AHEAD = 1
SMEM = pl.BlockSpec(memory_space=pltpu.SMEM)
VMEM = pl.BlockSpec(memory_space=pltpu.VMEM)
HBM = pl.BlockSpec(memory_space=pltpu.HBM)
ANY = pl.BlockSpec(memory_space=pl.ANY)
NN = ((1,), (0,))
NT = ((1,), (1,))


def grant(mib):
    return pltpu.CompilerParams(vmem_limit_bytes=mib * MIB)


def mxu(a, b, dims=NN):
    return lax.dot_general(a, b, (dims, ((), ())), preferred_element_type=jnp.float32)


def iota(shape, dim):
    return lax.broadcasted_iota(jnp.int32, shape, dim)


def whole(values):
    return values.astype(jnp.int32).astype(jnp.float32)


def tile_of(n):
    return slice(n * LANES, (n + 1) * LANES)


def layout(owners, pos_ref, decay_ref, lengths_ref):
    heads, rows = decay_ref.shape
    unit = rows // (2 * owners)
    pos_row = pos_ref[...].astype(jnp.float32)
    pos_col = jnp.transpose(jnp.broadcast_to(pos_row, (LANES, rows)))[:, 0:1]
    rank = jnp.sum((pos_col < pos_row).astype(jnp.float32), axis=0, keepdims=True)
    order = (iota((rows, rows), 0).astype(jnp.float32) == rank).astype(jnp.bfloat16)
    spare = jnp.zeros((AUX - 1 - heads, rows), jnp.float32)
    aux = jnp.concatenate(
        [decay_ref[...].astype(jnp.float32), spare, whole(pos_row * (1.0 / unit))], axis=0
    ).astype(jnp.bfloat16)
    by_row = mxu(aux, order, NT)
    by_col = mxu(order, aux, NT)
    units = by_row[AUX - 1 : AUX, :]
    per_owner = 1.0 / (rows // unit)
    owner_row, owner_col = whole(units * per_owner), whole(by_col[:, AUX - 1 : AUX] * per_owner)
    place = units.astype(jnp.int32) * unit + lax.rem(iota((1, rows), 1), unit)
    decay = by_row
    end = 0
    for j in range(lengths_ref.shape[0] - 1):
        end = end + lengths_ref[j]
        decay = jnp.where(place == end, CUT, decay)
    return order, decay.astype(jnp.bfloat16), units, owner_row, owner_col


def half_copies(sources, targets, sems, span):
    copies = [
        pltpu.make_async_copy(source.at[:, span], target, sems.at[n])
        for n, (source, target) in enumerate(zip(sources, targets))
    ]
    for copy in copies:
        copy.start()
    return copies


def states_kernel(owners, half, me_ref, pos_ref, decay_ref, lengths_ref, k_hbm, v_hbm, *refs):
    outs, (k_in, v_in, held, sems) = refs[:owners], refs[owners:]
    rows, width = k_in.shape
    copies = half_copies((k_hbm, v_hbm), (k_in, v_in), sems, pl.ds(half * width, width))
    order, decay, units, owner_row, owner_col = layout(owners, pos_ref, decay_ref, lengths_ref)
    after = (iota((rows, rows), 0) > iota((rows, rows), 1)) & (owner_col == owner_row)
    toward = jnp.exp(mxu(decay, after.astype(jnp.bfloat16)))
    of_owner = [owner_row == float(o) for o in range(owners)]
    line = iota((4 * owners, LANES), 0)
    marks = jnp.zeros((4 * owners, LANES), jnp.float32)
    sums = []
    for o in range(owners):
        first = jnp.min(jnp.where(of_owner[o], units, 1e9), axis=1, keepdims=True)
        marks = jnp.where(line == 3 * owners + o, first, marks)
        rest = jnp.sum(
            jnp.where(of_owner[o], decay.astype(jnp.float32), 0.0), axis=1, keepdims=True
        )
        for part in range(3):
            short = rest.astype(jnp.bfloat16).astype(jnp.float32)
            sums.append((part * owners + o, short))
            rest = rest - short
    copies[0].wait()
    turned = jnp.transpose(mxu(order, k_in[...]))
    copies[1].wait()
    v = mxu(order, v_in[...]).astype(jnp.bfloat16)
    for n in range(owners):
        h = half * owners + n
        k = turned[tile_of(n), :] * toward[h : h + 1, :]
        split = jnp.concatenate([jnp.where(own, k, 0.0) for own in of_owner], axis=0)
        held[n, :width, :] = mxu(split.astype(jnp.bfloat16), v[:, tile_of(n)]).astype(
            jnp.bfloat16
        )
        block = marks
        for at, short in sums:
            block = jnp.where(line == at, short[h : h + 1, :], block)
        held[n, width:, :] = block.astype(jnp.bfloat16)
    for s in range(owners):
        outs[s][...] = held[lax.rem(me_ref[0] + s, owners)]


def states(owners, half, me, positions, decays, lengths, keys, values):
    rows = keys.shape[0]
    width = owners * LANES
    out = jax.ShapeDtypeStruct((width + 4 * owners, LANES), jnp.bfloat16)
    result = pl.pallas_call(
        functools.partial(states_kernel, owners, half),
        out_shape=[out] * owners,
        in_specs=[SMEM, VMEM, VMEM, SMEM, HBM, HBM],
        out_specs=[VMEM] * owners,
        scratch_shapes=[
            pltpu.VMEM((rows, width), jnp.bfloat16),
            pltpu.VMEM((rows, width), jnp.bfloat16),
            pltpu.VMEM((owners, *out.shape), jnp.bfloat16),
            pltpu.SemaphoreType.DMA((2,)),
        ],
        compiler_params=grant(60),
        cost_estimate=pl.CostEstimate(flops=6 * rows * rows * width, bytes_accessed=rows * width * 6, transcendentals=0),
        name="run_states",
    )(me, positions, decays, lengths, keys, values)
    return list(result)


def inside_kernel(owners, half, pos_ref, decay_ref, lengths_ref, q_hbm, k_hbm, v_hbm, *refs):
    q_out, out, q_in, k_in, v_in, sems = refs
    rows, width = q_in.shape
    span = pl.ds(half * width, width)
    copies = half_copies((q_hbm, k_hbm, v_hbm), (q_in, k_in, v_in), sems, span)
    order, decay, _, owner_row, owner_col = layout(owners, pos_ref, decay_ref, lengths_ref)
    seen = (iota((rows, rows), 0) >= iota((rows, rows), 1)) & (owner_col == owner_row)
    counted = seen.astype(jnp.bfloat16)
    total_row, total_col = mxu(decay, counted, NT), mxu(counted, decay, NT)
    reach = jnp.exp(total_col)
    band = -(-(3 * rows // (2 * owners)) // LANES) * LANES
    for copy in copies:
        copy.wait()
    for source in (q_in, k_in, v_in):
        source[...] = mxu(order, source[...]).astype(jnp.bfloat16)
    for n in range(owners):
        h = half * owners + n
        cols = tile_of(n)
        q_out[:, cols] = (q_in[:, cols].astype(jnp.float32) * reach[:, h : h + 1]).astype(
            jnp.bfloat16
        )
        for top in range(0, rows, LANES):
            here = slice(top, top + LANES)
            past = slice(max(0, top - band), top + LANES)
            gap = total_col[here, h : h + 1] - total_row[h : h + 1, past]
            table = jnp.exp(jnp.where(seen[here, past], gap, -1e30))
            scores = mxu(q_in[here, cols], k_in[past, cols], NT) * table
            out[here, cols] = mxu(scores.astype(jnp.bfloat16), v_in[past, cols])


def inside(owners, half, positions, decays, lengths, queries, keys, values):
    rows = queries.shape[0]
    shape = (rows, owners * LANES)
    return pl.pallas_call(
        functools.partial(inside_kernel, owners, half),
        out_shape=[
            jax.ShapeDtypeStruct(shape, jnp.bfloat16),
            jax.ShapeDtypeStruct(shape, jnp.float32),
        ],
        in_specs=[VMEM, VMEM, SMEM, HBM, HBM, HBM],
        out_specs=[VMEM, VMEM],
        scratch_shapes=[pltpu.VMEM(shape, jnp.bfloat16)] * 3 + [pltpu.SemaphoreType.DMA((3,))],
        compiler_params=grant(24),
        cost_estimate=pl.CostEstimate(flops=6 * rows * rows * shape[1], bytes_accessed=rows * shape[1] * 12, transcendentals=owners * rows * rows),
        name="attend_inside_runs",
    )(positions, decays, lengths, queries, keys, values)


def chain_kernel(owners, *refs):
    blocks, outs = refs[:owners], refs[owners:]
    size = owners * LANES + 4 * owners
    for half in range(blocks[0].shape[0] // size):
        base = half * size
        marks = [b[base + owners * LANES : base + size, :].astype(jnp.float32) for b in blocks]
        state = jnp.zeros((LANES, LANES), jnp.float32)
        for o in range(owners):
            starts = [m[3 * owners + o : 3 * owners + o + 1, :] for m in marks]
            keeps = [
                jnp.exp(sum(m[p * owners + o : p * owners + o + 1, :] for p in range(3)))
                for m in marks
            ]
            ranks = [sum((other < own).astype(jnp.float32) for other in starts) for own in starts]
            runs = [b[base + o * LANES : base + (o + 1) * LANES, :] for b in blocks]
            before = []
            for place in range(owners):
                run, keep = runs[-1], keeps[-1]
                for s in range(owners - 1):
                    chosen = ranks[s] == float(place)
                    run = jnp.where(chosen, runs[s], run)
                    keep = jnp.where(chosen, keeps[s], keep)
                before.append(state.astype(jnp.bfloat16))
                state = keep * state + run.astype(jnp.float32)
            for s in range(owners):
                entry = before[-1]
                for place in range(owners - 1):
                    entry = jnp.where(ranks[s] == float(place), before[place], entry)
                row = half * owners * LANES + o * LANES
                outs[s][row : row + LANES, :] = entry


def chain(owners, blocks):
    size = owners * LANES + 4 * owners
    rows = blocks[0].shape[0] // size * owners * LANES
    return pl.pallas_call(
        functools.partial(chain_kernel, owners),
        out_shape=[jax.ShapeDtypeStruct((rows, LANES), jnp.bfloat16)] * owners,
        in_specs=[VMEM] * owners,
        out_specs=[VMEM] * owners,
        compiler_params=grant(12),
        cost_estimate=pl.CostEstimate(flops=owners * rows * LANES * 8, bytes_accessed=owners * rows * LANES * 4, transcendentals=0),
        name="chain_states",
    )(*blocks)


def finish_kernel(owners, me_ref, bounds_ref, gain_ref, q_ref, inside_ref, *refs):
    entries, outs, (held, normed) = refs[:owners], refs[owners:-2], refs[-2:]
    rows = q_ref.shape[0]
    unit = rows // (2 * owners)
    for s in range(owners):
        held[lax.rem(me_ref[0] + s, owners)] = entries[s][...]
    row = iota((rows, LANES), 0)
    mine = []
    for o in range(owners):
        top = bounds_ref[o + 1] if o + 1 < owners else rows
        mine.append((row >= bounds_ref[o]) & (row < top))
    for h in range(owners):
        q = q_ref[:, tile_of(h)]
        spread = jnp.concatenate([jnp.where(own, q, jnp.zeros_like(q)) for own in mine], axis=1)
        out = inside_ref[:, tile_of(h)] + mxu(spread, held[h])
        scale = lax.rsqrt(jnp.mean(out * out, axis=1, keepdims=True) + 1e-06)
        normed[:rows, tile_of(h)] = (out * scale * gain_ref[:, tile_of(h)]).astype(jnp.bfloat16)
    normed[rows:, :] = jnp.zeros((normed.shape[0] - rows, normed.shape[1]), jnp.bfloat16)
    for s in range(owners):
        start = pl.multiple_of(bounds_ref[lax.rem(me_ref[0] + s, owners)], unit)
        outs[s][...] = normed[pl.ds(start, 3 * unit), :]


def finish(owners, me, bounds, gain, scaled, within, entries):
    rows, width = scaled.shape
    unit = rows // (2 * owners)
    out = jax.ShapeDtypeStruct((3 * unit, width), jnp.bfloat16)
    return pl.pallas_call(
        functools.partial(finish_kernel, owners),
        out_shape=[out] * owners,
        in_specs=[SMEM, SMEM] + [VMEM] * (3 + owners),
        out_specs=[VMEM] * owners,
        scratch_shapes=[
            pltpu.VMEM((owners, owners * LANES, LANES), jnp.bfloat16),
            pltpu.VMEM((rows + 2 * unit, width), jnp.bfloat16),
        ],
        compiler_params=grant(20),
        cost_estimate=pl.CostEstimate(flops=2 * rows * width * width, bytes_accessed=rows * width * 10, transcendentals=0),
        name="finish_heads",
    )(me, bounds, gain, scaled, within, *entries)


def gather_kernel(owners, me_ref, starts_ref, *refs):
    runs, out = refs[:owners], refs[-1]
    unit = runs[0].shape[0] // 3
    per_owner = out.shape[0] // unit
    firsts = [starts_ref[s * owners + me_ref[0]] - me_ref[0] * per_owner for s in range(owners)]
    for s in range(owners):
        after = jnp.int32(per_owner)
        for other in firsts:
            after = jnp.where((other > firsts[s]) & (other < after), other, after)
        out[pl.ds(pl.multiple_of(firsts[s] * unit, unit), unit), :] = runs[s][:unit, :]

        @pl.when(after - firsts[s] > 1)
        def _(s=s):
            to = pl.multiple_of((firsts[s] + 1) * unit, unit)
            out[pl.ds(to, 2 * unit), :] = runs[s][unit:, :]


def gather_rows(owners, rows, me, starts, runs, tokens):
    width = runs[0].shape[1]
    return pl.pallas_call(
        functools.partial(gather_kernel, owners),
        out_shape=jax.ShapeDtypeStruct((rows, width), jnp.bfloat16),
        in_specs=[SMEM, SMEM] + [VMEM] * owners + [ANY] * len(tokens),
        out_specs=VMEM,
        compiler_params=grant(8),
        cost_estimate=pl.CostEstimate(flops=0, bytes_accessed=rows * width * 5, transcendentals=0),
        name="gather_own_rows",
    )(me, starts, *runs, *tokens)


def weight_rows(mine_ref, weight, places, depths):
    rows = []
    for (flip, first), depth in zip(places, depths):
        top = (mine_ref[0] ^ flip) * mine_ref[1] + first * LANES
        rows.append(weight.at[pl.ds(pl.multiple_of(top, LANES), depth), :])
    return rows


def fetch_rows(mine_ref, weight, places, depths, stacked, sems):
    at = 0
    copies = []
    for n, rows in enumerate(weight_rows(mine_ref, weight, places, depths)):
        copies.append(
            pltpu.make_async_copy(rows, stacked.at[pl.ds(at, depths[n]), :], sems.at[n])
        )
        copies[-1].start()
        at += depths[n]
    return copies


def hold_kernel(places, depths, mine_ref, weight, out, token, sems):
    token[...] = jnp.zeros_like(token)
    for copy in fetch_rows(mine_ref, weight, places, depths, out, sems):
        copy.wait()


def hold_rows(mine, weight, places, depths):
    return pl.pallas_call(
        functools.partial(hold_kernel, places, depths),
        out_shape=[
            pltpu.VMEM((sum(depths), weight.shape[1]), weight.dtype),
            jax.ShapeDtypeStruct((8, LANES), jnp.float32),
        ],
        in_specs=[SMEM, HBM],
        out_specs=[VMEM, VMEM],
        scratch_shapes=[pltpu.SemaphoreType.DMA((len(places),))],
        compiler_params=grant(4),
        name="hold_weight",
    )(mine, pltpu.with_memory_space_constraint(weight, pltpu.HBM))


def project_kernel(places, carried, mine_ref, *refs):
    count = len(places)
    parts, weight, rest = refs[:count], refs[count], refs[count + 1 :]
    out, token, stacked, sems = rest[-4:]
    depths = [part.shape[1] for part in parts]
    token[...] = jnp.zeros_like(token)
    for copy in fetch_rows(mine_ref, weight, places, depths, stacked, sems):
        copy.wait()
    rows = out.shape[0]
    tile = math.gcd(rows, LANES)
    for n in range(rows // tile):
        span = slice(n * tile, (n + 1) * tile)
        total = rest[0][span, :] if carried else None
        at = 0
        for part in parts:
            depth = part.shape[1]
            term = mxu(part[span, :], stacked[at : at + depth, :])
            total = term if total is None else total + term
            at += depth
        out[span, :] = total


def project(mine, places, parts, weight, carried):
    rows, width = parts[0].shape[0], weight.shape[1]
    depth = sum(part.shape[1] for part in parts)
    extra = [] if carried is None else [pltpu.with_memory_space_constraint(carried, pltpu.VMEM)]
    return pl.pallas_call(
        functools.partial(project_kernel, places, carried is not None),
        out_shape=[
            pltpu.VMEM((rows, width), jnp.float32),
            jax.ShapeDtypeStruct((8, LANES), jnp.float32),
        ],
        in_specs=[SMEM] + [VMEM] * len(parts) + [HBM] + [VMEM] * len(extra),
        out_specs=[VMEM, VMEM],
        scratch_shapes=[
            pltpu.VMEM((depth, width), jnp.bfloat16),
            pltpu.SemaphoreType.DMA((len(parts),)),
        ],
        compiler_params=grant(20),
        name="project",
    )(mine, *parts, pltpu.with_memory_space_constraint(weight, pltpu.HBM), *extra)


def project_more_kernel(part, held, carried, _, out, token):
    token[...] = jnp.zeros_like(token)
    rows = out.shape[0]
    tile = math.gcd(rows, LANES)
    for n in range(rows // tile):
        span = slice(n * tile, (n + 1) * tile)
        out[span, :] = carried[span, :] + mxu(part[span, :], held[...])


def project_more(part, held, carried, token):
    rows, width = carried.shape
    held, carried = (pltpu.with_memory_space_constraint(x, pltpu.VMEM) for x in (held, carried))
    return pl.pallas_call(
        project_more_kernel,
        out_shape=[
            pltpu.VMEM((rows, width), jnp.float32),
            jax.ShapeDtypeStruct((8, LANES), jnp.float32),
        ],
        in_specs=[VMEM] * 3 + [ANY],
        out_specs=[VMEM, VMEM],
        compiler_params=grant(8),
        name="project_more",
    )(part, held, carried, token)


def project_last_kernel(count, *refs):
    parts, (held, carried, _, out, tiles, sems) = refs[:count], refs[count:]
    rows = tiles.shape[0]
    tile = math.gcd(rows, LANES)
    stores = []
    for n in range(rows // tile):
        span = slice(n * tile, (n + 1) * tile)
        total = carried[span, :]
        at = 0
        for part in parts:
            depth = part.shape[1]
            total = total + mxu(part[span, :], held[at : at + depth, :])
            at += depth
        tiles[span, :] = total.astype(tiles.dtype)
        stores.append(
            pltpu.make_async_copy(tiles.at[span, :], out.at[span, :], sems.at[n])
        )
        stores[-1].start()
    for store in stores:
        store.wait()


def project_last(parts, held, carried, token):
    rows, width = carried.shape
    held, carried = (
        pltpu.with_memory_space_constraint(x, pltpu.VMEM) for x in (held, carried)
    )
    return pl.pallas_call(
        functools.partial(project_last_kernel, len(parts)),
        out_shape=pltpu.HBM((rows, width), jnp.bfloat16),
        in_specs=[VMEM] * (len(parts) + 2) + [ANY],
        out_specs=HBM,
        scratch_shapes=[
            pltpu.VMEM((rows, width), jnp.bfloat16),
            pltpu.SemaphoreType.DMA((rows // math.gcd(rows, LANES),)),
        ],
        compiler_params=grant(8),
        name="project_last",
    )(*parts, held, carried, token)


def shift_pairs(count, shift):
    return [(a, (a + shift) % count) for a in range(count)]


def exchange(owners, blocks, way):
    return [blocks[0]] + [
        lax.ppermute(blocks[s], "ctx", shift_pairs(owners, way * s)) for s in range(1, owners)
    ]


def local_by_runs(
    queries, keys, values, log_decay, arrival_positions, prompt_lengths, norm_gain, out_weight
):
    rows, width = queries.shape
    heads = log_decay.shape[1]
    owners = lax.axis_size("ctx")
    columns = lax.axis_size("head")
    mine = lax.axis_index("head")
    me = lax.axis_index("ctx").astype(jnp.int32).reshape(1)
    positions, decays = arrival_positions[None, :], log_decay.T
    halves = heads // owners
    depth = owners * LANES
    queries, keys, values = (
        pltpu.with_memory_space_constraint(x, pltpu.HBM) for x in (queries, keys, values)
    )
    gain = norm_gain.reshape(halves, 1, depth)
    blocks = []
    begun = positions
    for half in range(halves):
        sent = states(owners, half, me, begun, decays, prompt_lengths, keys, values)
        sent[0], begun = lax.optimization_barrier((sent[0], begun))
        if half:
            sent[-1], blocks[-1][1] = lax.optimization_barrier((sent[-1], blocks[-1][1]))
        blocks.append(exchange(owners, sent, 1))
    within = [inside(owners, 0, positions, decays, prompt_lengths, queries, keys, values)]
    blocks[0], within = lax.optimization_barrier((blocks[0], within))
    lines = rows * jnp.arange(owners, dtype=jnp.int32)
    bounds = jnp.sum((arrival_positions[:, None] < lines[None, :]).astype(jnp.int32), axis=0)
    first_mark = depth + 3 * owners
    starts = jnp.concatenate([b[first_mark : first_mark + owners, 0] for b in blocks[0]])
    starts = starts.astype(jnp.int32)
    entries = []
    for half in range(halves):
        linked = chain(owners, blocks[half])
        entries.append(exchange(owners, linked, -1))
    begun = positions
    for half in range(1, halves):
        entries[0][1], begun = lax.optimization_barrier((entries[0][1], begun))
        within.append(inside(owners, half, begun, decays, prompt_lengths, queries, keys, values))
    entries[0], within = lax.optimization_barrier((entries[0], within))

    def flip_head(part, flip):
        return lax.ppermute(part, "head", [(a, a ^ flip) for a in range(columns)])

    runs = []
    for half in range(halves):
        sent = finish(owners, me, bounds, gain[half], *within[half], entries[half])
        runs.append(exchange(owners, sent, 1))
    scalars = jnp.stack([mine, width]).astype(jnp.int32)
    far_columns = range(2, columns, 2)
    group, total, tokens = [], None, []
    crossed = []
    for half in range(halves):
        first = half * owners
        last = half == halves - 1
        if not last:
            runs[half], runs[half + 1][1] = lax.optimization_barrier(
                (runs[half], runs[half + 1][1])
            )
        elif group:
            total, token = project(
                scalars, [at for at, _ in group], [part for _, part in group], out_weight, None
            )
            tokens.append(token)
            group = []
        if last:
            helds = []
            for far in far_columns:
                for flip in (far, far + 1):
                    held, token = hold_rows(scalars, out_weight, [(flip, first)], [depth])
                    helds.append(held)
                    tokens.append(token)
        normed = gather_rows(owners, rows, me, starts, runs[half], tokens)
        if last:
            moved, normed = lax.optimization_barrier(([part for _, _, part in crossed], normed))
            crossed = [(far, at, part) for (far, at, _), part in zip(crossed, moved)]
        group += [((0, first), normed), ((1, first), flip_head(normed, 1))]
        across = [flip_head(normed, far) for far in far_columns]
        if last:
            for far, at, part in crossed:
                group += [((far, at), part), ((far + 1, at), flip_head(part, 1))]
            total, token = project(
                scalars, [at for at, _ in group], [part for _, part in group], out_weight, total
            )
            across[0], token = lax.optimization_barrier((across[0], token))
            group = []
            for far, part in zip(far_columns, across):
                group += [((far, first), part), ((far + 1, first), flip_head(part, 1))]
        else:
            crossed += [(far, first, part) for far, part in zip(far_columns, across)]
    for (_, part), held in zip(group[:-1], helds[:-1]):
        total, token = project_more(part, held, total, token)
    return project_last([group[-1][1]], helds[-1], total, token)


def split_terms(source):
    upper_part = source.astype(jnp.bfloat16)
    lower_part = (source - upper_part.astype(jnp.float32)).astype(jnp.bfloat16)
    return (upper_part, lower_part)


def paired_einsum(form, wide_operand, narrow_operand, wide_first):
    upper_part, lower_part = split_terms(wide_operand)
    if wide_first:
        return jnp.einsum(
            form, upper_part, narrow_operand, preferred_element_type=jnp.float32
        ) + jnp.einsum(form, lower_part, narrow_operand, preferred_element_type=jnp.float32)
    return jnp.einsum(
        form, narrow_operand, upper_part, preferred_element_type=jnp.float32
    ) + jnp.einsum(form, narrow_operand, lower_part, preferred_element_type=jnp.float32)


def block_terms(run_state, last_seg, block_q, block_k, block_v, block_cum, block_seg):
    linked = block_seg == last_seg
    reach_back = jnp.where(linked[:, None], jnp.exp(block_cum), 0.0)
    earlier = paired_einsum("thd,hde->the", run_state, block_q, False) * reach_back[:, :, None]
    block_rows = block_seg.shape[0]
    order_ok = jnp.arange(block_rows)[:, None] >= jnp.arange(block_rows)[None, :]
    allowed = order_ok & (block_seg[:, None] == block_seg[None, :])
    by_head = block_cum.T
    spread = by_head[:, :, None] - by_head[:, None, :]
    decay_table = jnp.where(allowed[None], jnp.exp(jnp.where(allowed[None], spread, 0.0)), 0.0)
    scores = jnp.einsum("thd,shd->hts", block_q, block_k, preferred_element_type=jnp.float32)
    inside = paired_einsum("hts,shd->thd", scores * decay_table, block_v, True)
    end_seg = block_seg[-1]
    toward = jnp.where(
        (block_seg == end_seg)[:, None], jnp.exp(block_cum[-1][None, :] - block_cum), 0.0
    )
    local_state = paired_einsum(
        "shd,she->hde", block_k.astype(jnp.float32) * toward[:, :, None], block_v, True
    )
    keep_factor = jnp.where(jnp.all(linked), jnp.exp(block_cum[-1]), 0.0)
    new_state = keep_factor[:, None, None] * run_state + local_state
    return (earlier + inside, new_state)


def attend(own_q, own_k, own_v, cumulative, segment, run_state, last_seg):
    block_out, run_state = block_terms(
        run_state, last_seg, own_q, own_k, own_v, cumulative, segment
    )
    return (block_out, run_state)


def carried_state(factor, end_state):
    owner_count = lax.axis_size("ctx")
    my_index = lax.axis_index("ctx")
    factors, states = (
        lax.all_gather(factor[None].astype(jnp.bfloat16), "ctx", axis=0, tiled=True).astype(
            jnp.float32
        ),
        lax.all_gather(end_state[None].astype(jnp.bfloat16), "ctx", axis=0, tiled=True).astype(
            jnp.float32
        ),
    )
    index_line = jnp.arange(owner_count)
    between = (index_line[None, :] > index_line[:, None]) & (index_line[None, :] < my_index)
    chain_weights = jnp.prod(jnp.where(between[:, :, None], factors[None, :, :], 1.0), axis=1)
    chain_weights = chain_weights * (index_line < my_index)[:, None].astype(jnp.float32)
    return jnp.einsum("nh,nhde->hde", chain_weights, states, precision=lax.Precision.HIGHEST)


def local_by_rows(
    queries, keys, values, log_decay, arrival_positions, prompt_lengths, norm_gain, out_weight
):
    row_count = queries.shape[0]
    heads_here = log_decay.shape[1]
    head_width = queries.shape[1] // heads_here
    owner_count = lax.axis_size("ctx")
    my_index = lax.axis_index("ctx")
    capacity = 3 * (row_count // (2 * owner_count))
    slot_total = owner_count * capacity
    every_position = lax.all_gather(arrival_positions, "ctx", axis=0, tiled=True)
    target = arrival_positions // row_count
    hit_table = (target[:, None] == jnp.arange(owner_count)[None, :]).astype(jnp.int32)
    slot_index = jnp.sum((jnp.cumsum(hit_table, axis=0) - 1) * hit_table, axis=1)
    send_slot = target * capacity + slot_index
    send_onehot = (jnp.arange(slot_total)[:, None] == send_slot[None, :]).astype(jnp.bfloat16)

    def pack_rows(source):
        packed = jnp.dot(send_onehot, source, preferred_element_type=jnp.float32).astype(
            source.dtype
        )
        return packed.reshape(owner_count, capacity, source.shape[1])

    arrived = (
        lax.all_to_all(pack_rows(queries), "ctx", split_axis=0, concat_axis=0, tiled=True),
        lax.all_to_all(pack_rows(keys), "ctx", split_axis=0, concat_axis=0, tiled=True),
        lax.all_to_all(pack_rows(values), "ctx", split_axis=0, concat_axis=0, tiled=True),
        lax.all_to_all(pack_rows(log_decay), "ctx", split_axis=0, concat_axis=0, tiled=True),
    )
    layout = every_position.reshape(owner_count, row_count)
    own_rows = layout // row_count == my_index
    rank_index = jnp.cumsum(own_rows.astype(jnp.int32), axis=1) - 1
    source_slot = (jnp.arange(owner_count)[:, None] * capacity + rank_index).reshape(-1)
    wanted = my_index * row_count + jnp.arange(row_count, dtype=jnp.int32)
    matches = every_position[None, :] == wanted[:, None]
    slot_of_row = jnp.sum(jnp.where(matches, source_slot[None, :], 0), axis=1)
    receive_onehot = (slot_of_row[:, None] == jnp.arange(slot_total)[None, :]).astype(jnp.bfloat16)

    def unpack_rows(buffer):
        flat_buffer = buffer.reshape(slot_total, buffer.shape[2])
        return jnp.dot(receive_onehot, flat_buffer, preferred_element_type=jnp.float32).astype(
            buffer.dtype
        )

    own_q = unpack_rows(arrived[0]).reshape(row_count, heads_here, head_width)
    own_k = unpack_rows(arrived[1]).reshape(row_count, heads_here, head_width)
    own_v = unpack_rows(arrived[2]).reshape(row_count, heads_here, head_width)
    cumulative = jnp.cumsum(unpack_rows(arrived[3]).astype(jnp.float32), axis=0)
    positions = my_index * row_count + jnp.arange(row_count, dtype=jnp.int32)
    prompt_ends = jnp.cumsum(prompt_lengths)[:-1]
    segment = jnp.sum((positions[:, None] >= prompt_ends[None, :]).astype(jnp.int32), axis=1)
    opens_prompt = (positions[0] == 0) | jnp.any(positions[0] == prompt_ends)
    through = jnp.logical_not(opens_prompt) & jnp.all(segment == segment[0])
    factor = jnp.where(through, jnp.exp(cumulative[-1]), 0.0)
    entry_seg = jnp.where(opens_prompt, -1, segment[0])
    empty_state = jnp.zeros((heads_here, head_width, head_width), jnp.float32)
    attention, end_state = attend(
        own_q, own_k, own_v, cumulative, segment, empty_state, jnp.int32(-1)
    )
    incoming = carried_state(factor, end_state)
    reach_back = jnp.where((segment == entry_seg)[:, None], jnp.exp(cumulative), 0.0)
    attention = (
        attention + paired_einsum("thd,hde->the", incoming, own_q, False) * reach_back[:, :, None]
    )
    inv_scale = lax.rsqrt(jnp.mean(attention * attention, axis=-1, keepdims=True) + 1e-06)
    normed = (attention * inv_scale * norm_gain.reshape(heads_here, head_width)).astype(
        jnp.bfloat16
    )
    normed = normed.reshape(row_count, heads_here * head_width)
    projected = jnp.dot(
        lax.all_gather(normed, "head", axis=1, tiled=True),
        out_weight,
        preferred_element_type=jnp.float32,
    )
    return projected.astype(jnp.bfloat16)


def local(
    queries, keys, values, log_decay, arrival_positions, prompt_lengths, norm_gain, out_weight
):
    heads, owners = log_decay.shape[1], lax.axis_size("ctx")
    head_width = queries.shape[1] // heads
    unit = queries.shape[0] // (2 * owners)
    fits = heads % owners == 0 and heads < AUX and head_width == LANES
    fits = fits and queries.shape[0] % LANES == 0 and unit % 16 == 0 and owners % 4 == 0
    plan = local_by_runs if fits else local_by_rows
    return plan(
        queries, keys, values, log_decay, arrival_positions, prompt_lengths, norm_gain, out_weight
    )


def solution(mesh):
    return jax.shard_map(
        local,
        mesh=mesh,
        in_specs=(
            P(("groups", "ctx"), "head"),
            P(("groups", "ctx"), "head"),
            P(("groups", "ctx"), "head"),
            P(("groups", "ctx"), "head"),
            P(("groups", "ctx")),
            P("groups"),
            P("head"),
            P(None, "head"),
        ),
        out_specs=P(("groups", "ctx"), "head"),
        check_vma=False,
    )
```

```python
import functools
import math

import jax
import jax.numpy as jnp
from jax import lax
from jax.experimental import pallas as pl
from jax.experimental.pallas import tpu as pltpu
from jax.sharding import PartitionSpec as P


LANES = 128
AUX = 16
CUT = -256.0
MIB = 1024 * 1024
AHEAD = 1
SMEM = pl.BlockSpec(memory_space=pltpu.SMEM)
VMEM = pl.BlockSpec(memory_space=pltpu.VMEM)
HBM = pl.BlockSpec(memory_space=pltpu.HBM)
ANY = pl.BlockSpec(memory_space=pl.ANY)
NN = ((1,), (0,))
NT = ((1,), (1,))


def grant(mib):
    return pltpu.CompilerParams(vmem_limit_bytes=mib * MIB)


def mxu(a, b, dims=NN):
    return lax.dot_general(a, b, (dims, ((), ())), preferred_element_type=jnp.float32)


def iota(shape, dim):
    return lax.broadcasted_iota(jnp.int32, shape, dim)


def whole(values):
    return values.astype(jnp.int32).astype(jnp.float32)


def tile_of(n):
    return slice(n * LANES, (n + 1) * LANES)


def order_rows(pos_ref):
    rows = pos_ref.shape[1]
    pos_row = pos_ref[...].astype(jnp.float32)
    pos_col = jnp.transpose(jnp.broadcast_to(pos_row, (LANES, rows)))[:, 0:1]
    rank = jnp.sum((pos_col < pos_row).astype(jnp.float32), axis=0, keepdims=True)
    return (iota((rows, rows), 0).astype(jnp.float32) == rank).astype(jnp.bfloat16)


def layout(owners, order, pos_ref, decay_ref, lengths_ref):
    heads, rows = decay_ref.shape
    unit = rows // (2 * owners)
    pos_row = pos_ref[...].astype(jnp.float32)
    spare = jnp.zeros((AUX - 1 - heads, rows), jnp.float32)
    aux = jnp.concatenate(
        [decay_ref[...].astype(jnp.float32), spare, whole(pos_row * (1.0 / unit))], axis=0
    ).astype(jnp.bfloat16)
    by_row = mxu(aux, order, NT)
    by_col = mxu(order, aux, NT)
    units = by_row[AUX - 1 : AUX, :]
    per_owner = 1.0 / (rows // unit)
    owner_row, owner_col = whole(units * per_owner), whole(by_col[:, AUX - 1 : AUX] * per_owner)
    place = units.astype(jnp.int32) * unit + lax.rem(iota((1, rows), 1), unit)
    decay = by_row
    end = 0
    for j in range(lengths_ref.shape[0] - 1):
        end = end + lengths_ref[j]
        decay = jnp.where(place == end, CUT, decay)
    return decay.astype(jnp.bfloat16), units, owner_row, owner_col


def half_copies(sources, targets, sems, span):
    copies = [
        pltpu.make_async_copy(source.at[:, span], target, sems.at[n])
        for n, (source, target) in enumerate(zip(sources, targets))
    ]
    for copy in copies:
        copy.start()
    return copies


def states_kernel(owners, half, me_ref, pos_ref, decay_ref, lengths_ref, k_hbm, v_hbm, *refs):
    outs, (k_in, v_in, held, sems) = refs[:owners], refs[owners:]
    rows, width = k_in.shape
    copies = half_copies((k_hbm, v_hbm), (k_in, v_in), sems, pl.ds(half * width, width))
    order = order_rows(pos_ref)
    for copy in copies:
        copy.wait()
    turned = jnp.transpose(mxu(order, k_in[...]))
    v = mxu(order, v_in[...]).astype(jnp.bfloat16)
    decay, units, owner_row, owner_col = layout(owners, order, pos_ref, decay_ref, lengths_ref)
    after = (iota((rows, rows), 0) > iota((rows, rows), 1)) & (owner_col == owner_row)
    toward = jnp.exp(mxu(decay, after.astype(jnp.bfloat16)))
    of_owner = [owner_row == float(o) for o in range(owners)]
    line = iota((4 * owners, LANES), 0)
    marks = jnp.zeros((4 * owners, LANES), jnp.float32)
    sums = []
    for o in range(owners):
        first = jnp.min(jnp.where(of_owner[o], units, 1e9), axis=1, keepdims=True)
        marks = jnp.where(line == 3 * owners + o, first, marks)
        rest = jnp.sum(
            jnp.where(of_owner[o], decay.astype(jnp.float32), 0.0), axis=1, keepdims=True
        )
        for part in range(3):
            short = rest.astype(jnp.bfloat16).astype(jnp.float32)
            sums.append((part * owners + o, short))
            rest = rest - short
    for n in range(owners):
        h = half * owners + n
        k = turned[tile_of(n), :] * toward[h : h + 1, :]
        split = jnp.concatenate([jnp.where(own, k, 0.0) for own in of_owner], axis=0)
        held[n, :width, :] = mxu(split.astype(jnp.bfloat16), v[:, tile_of(n)]).astype(
            jnp.bfloat16
        )
        block = marks
        for at, short in sums:
            block = jnp.where(line == at, short[h : h + 1, :], block)
        held[n, width:, :] = block.astype(jnp.bfloat16)
    for s in range(owners):
        outs[s][...] = held[lax.rem(me_ref[0] + s, owners)]


def states(owners, half, me, positions, decays, lengths, keys, values):
    rows = keys.shape[0]
    width = owners * LANES
    out = jax.ShapeDtypeStruct((width + 4 * owners, LANES), jnp.bfloat16)
    result = pl.pallas_call(
        functools.partial(states_kernel, owners, half),
        out_shape=[out] * owners,
        in_specs=[SMEM, VMEM, VMEM, SMEM, HBM, HBM],
        out_specs=[VMEM] * owners,
        scratch_shapes=[
            pltpu.VMEM((rows, width), jnp.bfloat16),
            pltpu.VMEM((rows, width), jnp.bfloat16),
            pltpu.VMEM((owners, *out.shape), jnp.bfloat16),
            pltpu.SemaphoreType.DMA((2,)),
        ],
        compiler_params=grant(60),
        cost_estimate=pl.CostEstimate(flops=6 * rows * rows * width, bytes_accessed=rows * width * 6, transcendentals=0),
        name="run_states",
    )(me, positions, decays, lengths, keys, values)
    return list(result)


def inside_kernel(owners, half, pos_ref, decay_ref, lengths_ref, q_hbm, k_hbm, v_hbm, *refs):
    q_out, out, q_in, k_in, v_in, sems = refs
    rows, width = q_in.shape
    span = pl.ds(half * width, width)
    copies = half_copies((q_hbm, k_hbm, v_hbm), (q_in, k_in, v_in), sems, span)
    order = order_rows(pos_ref)
    for copy in copies:
        copy.wait()
    for source in (q_in, k_in, v_in):
        source[...] = mxu(order, source[...]).astype(jnp.bfloat16)
    decay, _, owner_row, owner_col = layout(owners, order, pos_ref, decay_ref, lengths_ref)
    seen = (iota((rows, rows), 0) >= iota((rows, rows), 1)) & (owner_col == owner_row)
    counted = seen.astype(jnp.bfloat16)
    total_row, total_col = mxu(decay, counted, NT), mxu(counted, decay, NT)
    reach = jnp.exp(total_col)
    band = -(-(3 * rows // (2 * owners)) // LANES) * LANES
    for n in range(owners):
        h = half * owners + n
        cols = tile_of(n)
        q_out[:, cols] = (q_in[:, cols].astype(jnp.float32) * reach[:, h : h + 1]).astype(
            jnp.bfloat16
        )
        for top in range(0, rows, LANES):
            here = slice(top, top + LANES)
            past = slice(max(0, top - band), top + LANES)
            gap = total_col[here, h : h + 1] - total_row[h : h + 1, past]
            table = jnp.exp(jnp.where(seen[here, past], gap, -1e30))
            scores = mxu(q_in[here, cols], k_in[past, cols], NT) * table
            out[here, cols] = mxu(scores.astype(jnp.bfloat16), v_in[past, cols])


def inside(owners, half, positions, decays, lengths, queries, keys, values):
    rows = queries.shape[0]
    shape = (rows, owners * LANES)
    return pl.pallas_call(
        functools.partial(inside_kernel, owners, half),
        out_shape=[
            jax.ShapeDtypeStruct(shape, jnp.bfloat16),
            jax.ShapeDtypeStruct(shape, jnp.float32),
        ],
        in_specs=[VMEM, VMEM, SMEM, HBM, HBM, HBM],
        out_specs=[VMEM, VMEM],
        scratch_shapes=[pltpu.VMEM(shape, jnp.bfloat16)] * 3 + [pltpu.SemaphoreType.DMA((3,))],
        compiler_params=grant(24),
        cost_estimate=pl.CostEstimate(flops=6 * rows * rows * shape[1], bytes_accessed=rows * shape[1] * 12, transcendentals=owners * rows * rows),
        name="attend_inside_runs",
    )(positions, decays, lengths, queries, keys, values)


def chain_kernel(owners, *refs):
    blocks, outs = refs[:owners], refs[owners:]
    size = owners * LANES + 4 * owners
    for half in range(blocks[0].shape[0] // size):
        base = half * size
        marks = [b[base + owners * LANES : base + size, :].astype(jnp.float32) for b in blocks]
        state = jnp.zeros((LANES, LANES), jnp.float32)
        for o in range(owners):
            starts = [m[3 * owners + o : 3 * owners + o + 1, :] for m in marks]
            keeps = [
                jnp.exp(sum(m[p * owners + o : p * owners + o + 1, :] for p in range(3)))
                for m in marks
            ]
            ranks = [sum((other < own).astype(jnp.float32) for other in starts) for own in starts]
            runs = [b[base + o * LANES : base + (o + 1) * LANES, :] for b in blocks]
            before = []
            for place in range(owners):
                run, keep = runs[-1], keeps[-1]
                for s in range(owners - 1):
                    chosen = ranks[s] == float(place)
                    run = jnp.where(chosen, runs[s], run)
                    keep = jnp.where(chosen, keeps[s], keep)
                before.append(state.astype(jnp.bfloat16))
                state = keep * state + run.astype(jnp.float32)
            for s in range(owners):
                entry = before[-1]
                for place in range(owners - 1):
                    entry = jnp.where(ranks[s] == float(place), before[place], entry)
                row = half * owners * LANES + o * LANES
                outs[s][row : row + LANES, :] = entry


def chain(owners, blocks):
    size = owners * LANES + 4 * owners
    rows = blocks[0].shape[0] // size * owners * LANES
    return pl.pallas_call(
        functools.partial(chain_kernel, owners),
        out_shape=[jax.ShapeDtypeStruct((rows, LANES), jnp.bfloat16)] * owners,
        in_specs=[VMEM] * owners,
        out_specs=[VMEM] * owners,
        compiler_params=grant(12),
        cost_estimate=pl.CostEstimate(flops=owners * rows * LANES * 8, bytes_accessed=owners * rows * LANES * 4, transcendentals=0),
        name="chain_states",
    )(*blocks)


def finish_kernel(owners, me_ref, bounds_ref, gain_ref, q_ref, inside_ref, *refs):
    entries, outs, (held, normed) = refs[:owners], refs[owners:-2], refs[-2:]
    rows = q_ref.shape[0]
    unit = rows // (2 * owners)
    for s in range(owners):
        held[lax.rem(me_ref[0] + s, owners)] = entries[s][...]
    row = iota((rows, LANES), 0)
    mine = []
    for o in range(owners):
        top = bounds_ref[o + 1] if o + 1 < owners else rows
        mine.append(((row >= bounds_ref[o]) & (row < top)).astype(jnp.bfloat16))
    for h in range(owners):
        q = q_ref[:, tile_of(h)]
        spread = jnp.concatenate([q * own for own in mine], axis=1)
        out = inside_ref[:, tile_of(h)] + mxu(spread, held[h])
        scale = lax.rsqrt(jnp.mean(out * out, axis=1, keepdims=True) + 1e-06)
        normed[:rows, tile_of(h)] = (out * scale * gain_ref[:, tile_of(h)]).astype(jnp.bfloat16)
    normed[rows:, :] = jnp.zeros((normed.shape[0] - rows, normed.shape[1]), jnp.bfloat16)
    for s in range(owners):
        start = pl.multiple_of(bounds_ref[lax.rem(me_ref[0] + s, owners)], unit)
        outs[s][...] = normed[pl.ds(start, 3 * unit), :]


def finish(owners, me, bounds, gain, scaled, within, entries):
    rows, width = scaled.shape
    unit = rows // (2 * owners)
    out = jax.ShapeDtypeStruct((3 * unit, width), jnp.bfloat16)
    return pl.pallas_call(
        functools.partial(finish_kernel, owners),
        out_shape=[out] * owners,
        in_specs=[SMEM, SMEM] + [VMEM] * (3 + owners),
        out_specs=[VMEM] * owners,
        scratch_shapes=[
            pltpu.VMEM((owners, owners * LANES, LANES), jnp.bfloat16),
            pltpu.VMEM((rows + 2 * unit, width), jnp.bfloat16),
        ],
        compiler_params=grant(20),
        cost_estimate=pl.CostEstimate(flops=2 * rows * width * width, bytes_accessed=rows * width * 10, transcendentals=0),
        name="finish_heads",
    )(me, bounds, gain, scaled, within, *entries)


def gather_kernel(owners, me_ref, starts_ref, *refs):
    runs, out = refs[:owners], refs[-1]
    unit = runs[0].shape[0] // 3
    per_owner = out.shape[0] // unit
    firsts = [starts_ref[s * owners + me_ref[0]] - me_ref[0] * per_owner for s in range(owners)]
    for s in range(owners):
        after = jnp.int32(per_owner)
        for other in firsts:
            after = jnp.where((other > firsts[s]) & (other < after), other, after)
        out[pl.ds(pl.multiple_of(firsts[s] * unit, unit), unit), :] = runs[s][:unit, :]

        @pl.when(after - firsts[s] > 1)
        def _(s=s):
            to = pl.multiple_of((firsts[s] + 1) * unit, unit)
            out[pl.ds(to, 2 * unit), :] = runs[s][unit:, :]


def gather_rows(owners, rows, me, starts, runs, tokens):
    width = runs[0].shape[1]
    return pl.pallas_call(
        functools.partial(gather_kernel, owners),
        out_shape=jax.ShapeDtypeStruct((rows, width), jnp.bfloat16),
        in_specs=[SMEM, SMEM] + [VMEM] * owners + [ANY] * len(tokens),
        out_specs=VMEM,
        compiler_params=grant(8),
        cost_estimate=pl.CostEstimate(flops=0, bytes_accessed=rows * width * 5, transcendentals=0),
        name="gather_own_rows",
    )(me, starts, *runs, *tokens)


def weight_rows(mine_ref, weight, places, depths):
    rows = []
    for (flip, first), depth in zip(places, depths):
        top = (mine_ref[0] ^ flip) * mine_ref[1] + first * LANES
        rows.append(weight.at[pl.ds(pl.multiple_of(top, LANES), depth), :])
    return rows


def fetch_rows(mine_ref, weight, places, depths, stacked, sems):
    at = 0
    copies = []
    for n, rows in enumerate(weight_rows(mine_ref, weight, places, depths)):
        copies.append(
            pltpu.make_async_copy(rows, stacked.at[pl.ds(at, depths[n]), :], sems.at[n])
        )
        copies[-1].start()
        at += depths[n]
    return copies


def hold_kernel(places, depths, mine_ref, weight, out, token, sems):
    token[...] = jnp.zeros_like(token)
    for copy in fetch_rows(mine_ref, weight, places, depths, out, sems):
        copy.wait()


def hold_rows(mine, weight, places, depths):
    return pl.pallas_call(
        functools.partial(hold_kernel, places, depths),
        out_shape=[
            pltpu.VMEM((sum(depths), weight.shape[1]), weight.dtype),
            jax.ShapeDtypeStruct((8, LANES), jnp.float32),
        ],
        in_specs=[SMEM, HBM],
        out_specs=[VMEM, VMEM],
        scratch_shapes=[pltpu.SemaphoreType.DMA((len(places),))],
        compiler_params=grant(4),
        name="hold_weight",
    )(mine, pltpu.with_memory_space_constraint(weight, pltpu.HBM))


def project_kernel(places, carried, mine_ref, *refs):
    count = len(places)
    parts, weight, rest = refs[:count], refs[count], refs[count + 1 :]
    out, token, stacked, sems = rest[-4:]
    depths = [part.shape[1] for part in parts]
    token[...] = jnp.zeros_like(token)
    for copy in fetch_rows(mine_ref, weight, places, depths, stacked, sems):
        copy.wait()
    rows = out.shape[0]
    tile = math.gcd(rows, LANES)
    for n in range(rows // tile):
        span = slice(n * tile, (n + 1) * tile)
        total = rest[0][span, :] if carried else None
        at = 0
        for part in parts:
            depth = part.shape[1]
            term = mxu(part[span, :], stacked[at : at + depth, :])
            total = term if total is None else total + term
            at += depth
        out[span, :] = total


def project(mine, places, parts, weight, carried):
    rows, width = parts[0].shape[0], weight.shape[1]
    depth = sum(part.shape[1] for part in parts)
    extra = [] if carried is None else [pltpu.with_memory_space_constraint(carried, pltpu.VMEM)]
    return pl.pallas_call(
        functools.partial(project_kernel, places, carried is not None),
        out_shape=[
            pltpu.VMEM((rows, width), jnp.float32),
            jax.ShapeDtypeStruct((8, LANES), jnp.float32),
        ],
        in_specs=[SMEM] + [VMEM] * len(parts) + [HBM] + [VMEM] * len(extra),
        out_specs=[VMEM, VMEM],
        scratch_shapes=[
            pltpu.VMEM((depth, width), jnp.bfloat16),
            pltpu.SemaphoreType.DMA((len(parts),)),
        ],
        compiler_params=grant(20),
        name="project",
    )(mine, *parts, pltpu.with_memory_space_constraint(weight, pltpu.HBM), *extra)


def project_more_kernel(part, held, carried, _, out, token):
    token[...] = jnp.zeros_like(token)
    rows = out.shape[0]
    tile = math.gcd(rows, LANES)
    for n in range(rows // tile):
        span = slice(n * tile, (n + 1) * tile)
        out[span, :] = carried[span, :] + mxu(part[span, :], held[...])


def project_more(part, held, carried, token):
    rows, width = carried.shape
    held, carried = (pltpu.with_memory_space_constraint(x, pltpu.VMEM) for x in (held, carried))
    return pl.pallas_call(
        project_more_kernel,
        out_shape=[
            pltpu.VMEM((rows, width), jnp.float32),
            jax.ShapeDtypeStruct((8, LANES), jnp.float32),
        ],
        in_specs=[VMEM] * 3 + [ANY],
        out_specs=[VMEM, VMEM],
        compiler_params=grant(8),
        name="project_more",
    )(part, held, carried, token)


def project_last_kernel(count, *refs):
    parts, (held, carried, _, out, tiles, sems) = refs[:count], refs[count:]
    rows = tiles.shape[0]
    tile = math.gcd(rows, LANES)
    stores = []
    for n in range(rows // tile):
        span = slice(n * tile, (n + 1) * tile)
        total = carried[span, :]
        at = 0
        for part in parts:
            depth = part.shape[1]
            total = total + mxu(part[span, :], held[at : at + depth, :])
            at += depth
        tiles[span, :] = total.astype(tiles.dtype)
        stores.append(
            pltpu.make_async_copy(tiles.at[span, :], out.at[span, :], sems.at[n])
        )
        stores[-1].start()
    for store in stores:
        store.wait()


def project_last(parts, held, carried, token):
    rows, width = carried.shape
    held, carried = (
        pltpu.with_memory_space_constraint(x, pltpu.VMEM) for x in (held, carried)
    )
    return pl.pallas_call(
        functools.partial(project_last_kernel, len(parts)),
        out_shape=pltpu.HBM((rows, width), jnp.bfloat16),
        in_specs=[VMEM] * (len(parts) + 2) + [ANY],
        out_specs=HBM,
        scratch_shapes=[
            pltpu.VMEM((rows, width), jnp.bfloat16),
            pltpu.SemaphoreType.DMA((rows // math.gcd(rows, LANES),)),
        ],
        compiler_params=grant(8),
        name="project_last",
    )(*parts, held, carried, token)


def shift_pairs(count, shift):
    return [(a, (a + shift) % count) for a in range(count)]


def exchange(owners, blocks, way):
    return [blocks[0]] + [
        lax.ppermute(blocks[s], "ctx", shift_pairs(owners, way * s)) for s in range(1, owners)
    ]


def local_by_runs(
    queries, keys, values, log_decay, arrival_positions, prompt_lengths, norm_gain, out_weight
):
    rows, width = queries.shape
    heads = log_decay.shape[1]
    owners = lax.axis_size("ctx")
    columns = lax.axis_size("head")
    mine = lax.axis_index("head")
    me = lax.axis_index("ctx").astype(jnp.int32).reshape(1)
    positions, decays = arrival_positions[None, :], log_decay.T
    halves = heads // owners
    depth = owners * LANES
    queries, keys, values = (
        pltpu.with_memory_space_constraint(x, pltpu.HBM) for x in (queries, keys, values)
    )
    gain = norm_gain.reshape(halves, 1, depth)
    blocks = []
    begun = positions
    for half in range(halves):
        sent = states(owners, half, me, begun, decays, prompt_lengths, keys, values)
        sent[0], begun = lax.optimization_barrier((sent[0], begun))
        if half:
            sent[-1], blocks[-1][1] = lax.optimization_barrier((sent[-1], blocks[-1][1]))
        blocks.append(exchange(owners, sent, 1))
    within = [inside(owners, 0, positions, decays, prompt_lengths, queries, keys, values)]
    blocks[0], within = lax.optimization_barrier((blocks[0], within))
    lines = rows * jnp.arange(owners, dtype=jnp.int32)
    bounds = jnp.sum((arrival_positions[:, None] < lines[None, :]).astype(jnp.int32), axis=0)
    first_mark = depth + 3 * owners
    starts = jnp.concatenate([b[first_mark : first_mark + owners, 0] for b in blocks[0]])
    starts = starts.astype(jnp.int32)
    entries = []
    for half in range(halves):
        linked = chain(owners, blocks[half])
        entries.append(exchange(owners, linked, -1))
    begun = positions
    for half in range(1, halves):
        entries[0][1], begun = lax.optimization_barrier((entries[0][1], begun))
        within.append(inside(owners, half, begun, decays, prompt_lengths, queries, keys, values))
    entries[0], within = lax.optimization_barrier((entries[0], within))

    def flip_head(part, flip):
        return lax.ppermute(part, "head", [(a, a ^ flip) for a in range(columns)])

    runs = []
    for half in range(halves):
        sent = finish(owners, me, bounds, gain[half], *within[half], entries[half])
        runs.append(exchange(owners, sent, 1))
    scalars = jnp.stack([mine, width]).astype(jnp.int32)
    far_columns = range(2, columns, 2)
    group, total, tokens = [], None, []
    crossed = []
    for half in range(halves):
        first = half * owners
        last = half == halves - 1
        if not last:
            runs[half], runs[half + 1][1] = lax.optimization_barrier(
                (runs[half], runs[half + 1][1])
            )
        elif group:
            total, token = project(
                scalars, [at for at, _ in group], [part for _, part in group], out_weight, None
            )
            tokens.append(token)
            group = []
        if last:
            helds = []
            for far in far_columns:
                for flip in (far, far + 1):
                    held, token = hold_rows(scalars, out_weight, [(flip, first)], [depth])
                    helds.append(held)
                    tokens.append(token)
        normed = gather_rows(owners, rows, me, starts, runs[half], tokens)
        if last:
            moved, normed = lax.optimization_barrier(([part for _, _, part in crossed], normed))
            crossed = [(far, at, part) for (far, at, _), part in zip(crossed, moved)]
        group += [((0, first), normed), ((1, first), flip_head(normed, 1))]
        across = [flip_head(normed, far) for far in far_columns]
        if last:
            for far, at, part in crossed:
                group += [((far, at), part), ((far + 1, at), flip_head(part, 1))]
            total, token = project(
                scalars, [at for at, _ in group], [part for _, part in group], out_weight, total
            )
            across[0], token = lax.optimization_barrier((across[0], token))
            group = []
            for far, part in zip(far_columns, across):
                group += [((far, first), part), ((far + 1, first), flip_head(part, 1))]
        else:
            crossed += [(far, first, part) for far, part in zip(far_columns, across)]
    for (_, part), held in zip(group[:-1], helds[:-1]):
        total, token = project_more(part, held, total, token)
    return project_last([group[-1][1]], helds[-1], total, token)


def split_terms(source):
    upper_part = source.astype(jnp.bfloat16)
    lower_part = (source - upper_part.astype(jnp.float32)).astype(jnp.bfloat16)
    return (upper_part, lower_part)


def paired_einsum(form, wide_operand, narrow_operand, wide_first):
    upper_part, lower_part = split_terms(wide_operand)
    if wide_first:
        return jnp.einsum(
            form, upper_part, narrow_operand, preferred_element_type=jnp.float32
        ) + jnp.einsum(form, lower_part, narrow_operand, preferred_element_type=jnp.float32)
    return jnp.einsum(
        form, narrow_operand, upper_part, preferred_element_type=jnp.float32
    ) + jnp.einsum(form, narrow_operand, lower_part, preferred_element_type=jnp.float32)


def block_terms(run_state, last_seg, block_q, block_k, block_v, block_cum, block_seg):
    linked = block_seg == last_seg
    reach_back = jnp.where(linked[:, None], jnp.exp(block_cum), 0.0)
    earlier = paired_einsum("thd,hde->the", run_state, block_q, False) * reach_back[:, :, None]
    block_rows = block_seg.shape[0]
    order_ok = jnp.arange(block_rows)[:, None] >= jnp.arange(block_rows)[None, :]
    allowed = order_ok & (block_seg[:, None] == block_seg[None, :])
    by_head = block_cum.T
    spread = by_head[:, :, None] - by_head[:, None, :]
    decay_table = jnp.where(allowed[None], jnp.exp(jnp.where(allowed[None], spread, 0.0)), 0.0)
    scores = jnp.einsum("thd,shd->hts", block_q, block_k, preferred_element_type=jnp.float32)
    inside = paired_einsum("hts,shd->thd", scores * decay_table, block_v, True)
    end_seg = block_seg[-1]
    toward = jnp.where(
        (block_seg == end_seg)[:, None], jnp.exp(block_cum[-1][None, :] - block_cum), 0.0
    )
    local_state = paired_einsum(
        "shd,she->hde", block_k.astype(jnp.float32) * toward[:, :, None], block_v, True
    )
    keep_factor = jnp.where(jnp.all(linked), jnp.exp(block_cum[-1]), 0.0)
    new_state = keep_factor[:, None, None] * run_state + local_state
    return (earlier + inside, new_state)


def attend(own_q, own_k, own_v, cumulative, segment, run_state, last_seg):
    block_out, run_state = block_terms(
        run_state, last_seg, own_q, own_k, own_v, cumulative, segment
    )
    return (block_out, run_state)


def carried_state(factor, end_state):
    owner_count = lax.axis_size("ctx")
    my_index = lax.axis_index("ctx")
    factors, states = (
        lax.all_gather(factor[None].astype(jnp.bfloat16), "ctx", axis=0, tiled=True).astype(
            jnp.float32
        ),
        lax.all_gather(end_state[None].astype(jnp.bfloat16), "ctx", axis=0, tiled=True).astype(
            jnp.float32
        ),
    )
    index_line = jnp.arange(owner_count)
    between = (index_line[None, :] > index_line[:, None]) & (index_line[None, :] < my_index)
    chain_weights = jnp.prod(jnp.where(between[:, :, None], factors[None, :, :], 1.0), axis=1)
    chain_weights = chain_weights * (index_line < my_index)[:, None].astype(jnp.float32)
    return jnp.einsum("nh,nhde->hde", chain_weights, states, precision=lax.Precision.HIGHEST)


def local_by_rows(
    queries, keys, values, log_decay, arrival_positions, prompt_lengths, norm_gain, out_weight
):
    row_count = queries.shape[0]
    heads_here = log_decay.shape[1]
    head_width = queries.shape[1] // heads_here
    owner_count = lax.axis_size("ctx")
    my_index = lax.axis_index("ctx")
    capacity = 3 * (row_count // (2 * owner_count))
    slot_total = owner_count * capacity
    every_position = lax.all_gather(arrival_positions, "ctx", axis=0, tiled=True)
    target = arrival_positions // row_count
    hit_table = (target[:, None] == jnp.arange(owner_count)[None, :]).astype(jnp.int32)
    slot_index = jnp.sum((jnp.cumsum(hit_table, axis=0) - 1) * hit_table, axis=1)
    send_slot = target * capacity + slot_index
    send_onehot = (jnp.arange(slot_total)[:, None] == send_slot[None, :]).astype(jnp.bfloat16)

    def pack_rows(source):
        packed = jnp.dot(send_onehot, source, preferred_element_type=jnp.float32).astype(
            source.dtype
        )
        return packed.reshape(owner_count, capacity, source.shape[1])

    arrived = (
        lax.all_to_all(pack_rows(queries), "ctx", split_axis=0, concat_axis=0, tiled=True),
        lax.all_to_all(pack_rows(keys), "ctx", split_axis=0, concat_axis=0, tiled=True),
        lax.all_to_all(pack_rows(values), "ctx", split_axis=0, concat_axis=0, tiled=True),
        lax.all_to_all(pack_rows(log_decay), "ctx", split_axis=0, concat_axis=0, tiled=True),
    )
    layout = every_position.reshape(owner_count, row_count)
    own_rows = layout // row_count == my_index
    rank_index = jnp.cumsum(own_rows.astype(jnp.int32), axis=1) - 1
    source_slot = (jnp.arange(owner_count)[:, None] * capacity + rank_index).reshape(-1)
    wanted = my_index * row_count + jnp.arange(row_count, dtype=jnp.int32)
    matches = every_position[None, :] == wanted[:, None]
    slot_of_row = jnp.sum(jnp.where(matches, source_slot[None, :], 0), axis=1)
    receive_onehot = (slot_of_row[:, None] == jnp.arange(slot_total)[None, :]).astype(jnp.bfloat16)

    def unpack_rows(buffer):
        flat_buffer = buffer.reshape(slot_total, buffer.shape[2])
        return jnp.dot(receive_onehot, flat_buffer, preferred_element_type=jnp.float32).astype(
            buffer.dtype
        )

    own_q = unpack_rows(arrived[0]).reshape(row_count, heads_here, head_width)
    own_k = unpack_rows(arrived[1]).reshape(row_count, heads_here, head_width)
    own_v = unpack_rows(arrived[2]).reshape(row_count, heads_here, head_width)
    cumulative = jnp.cumsum(unpack_rows(arrived[3]).astype(jnp.float32), axis=0)
    positions = my_index * row_count + jnp.arange(row_count, dtype=jnp.int32)
    prompt_ends = jnp.cumsum(prompt_lengths)[:-1]
    segment = jnp.sum((positions[:, None] >= prompt_ends[None, :]).astype(jnp.int32), axis=1)
    opens_prompt = (positions[0] == 0) | jnp.any(positions[0] == prompt_ends)
    through = jnp.logical_not(opens_prompt) & jnp.all(segment == segment[0])
    factor = jnp.where(through, jnp.exp(cumulative[-1]), 0.0)
    entry_seg = jnp.where(opens_prompt, -1, segment[0])
    empty_state = jnp.zeros((heads_here, head_width, head_width), jnp.float32)
    attention, end_state = attend(
        own_q, own_k, own_v, cumulative, segment, empty_state, jnp.int32(-1)
    )
    incoming = carried_state(factor, end_state)
    reach_back = jnp.where((segment == entry_seg)[:, None], jnp.exp(cumulative), 0.0)
    attention = (
        attention + paired_einsum("thd,hde->the", incoming, own_q, False) * reach_back[:, :, None]
    )
    inv_scale = lax.rsqrt(jnp.mean(attention * attention, axis=-1, keepdims=True) + 1e-06)
    normed = (attention * inv_scale * norm_gain.reshape(heads_here, head_width)).astype(
        jnp.bfloat16
    )
    normed = normed.reshape(row_count, heads_here * head_width)
    projected = jnp.dot(
        lax.all_gather(normed, "head", axis=1, tiled=True),
        out_weight,
        preferred_element_type=jnp.float32,
    )
    return projected.astype(jnp.bfloat16)


def local(
    queries, keys, values, log_decay, arrival_positions, prompt_lengths, norm_gain, out_weight
):
    heads, owners = log_decay.shape[1], lax.axis_size("ctx")
    head_width = queries.shape[1] // heads
    unit = queries.shape[0] // (2 * owners)
    fits = heads % owners == 0 and heads < AUX and head_width == LANES
    fits = fits and queries.shape[0] % LANES == 0 and unit % 16 == 0 and owners % 4 == 0
    plan = local_by_runs if fits else local_by_rows
    return plan(
        queries, keys, values, log_decay, arrival_positions, prompt_lengths, norm_gain, out_weight
    )


def solution(mesh):
    return jax.shard_map(
        local,
        mesh=mesh,
        in_specs=(
            P(("groups", "ctx"), "head"),
            P(("groups", "ctx"), "head"),
            P(("groups", "ctx"), "head"),
            P(("groups", "ctx"), "head"),
            P(("groups", "ctx")),
            P("groups"),
            P("head"),
            P(None, "head"),
        ),
        out_specs=P(("groups", "ctx"), "head"),
        check_vma=False,
    )
```
